32 devices in a mesh: ctx: 16 (over z, y, x), head: 2 (over core).
Axes of the slice: x: 2, y: 2, z: 4, core: 2. Of those that a mesh axis runs over, the one named last changes fastest.
Arguments:
- queries: bfloat16 [2048, 3072], P('ctx', 'head'), may hold values from -6 to 6
- keys: bfloat16 [2048, 3072], P('ctx', 'head'), may hold values from -6 to 6
- values: bfloat16 [2048, 3072], P('ctx', 'head'), may hold values from -30 to 30
- decay_log: float32 [32, 2048], P('head', 'ctx'), may hold values from -1 to 0
- norm_gain: float32 [3072], P('head'), may hold values from 0.25 to 1.75
- out_grad: bfloat16 [2048, 3072], P('ctx', 'head'), may hold values from -6 to 6
- doc_lengths: int32 [16], replicated, may hold values from 1 to 512, 2048 in all
Outputs:
- attn_output: bfloat16 [2048, 3072], P('ctx', 'head')
- query_grad: bfloat16 [2048, 3072], P('ctx', 'head')
- key_grad: bfloat16 [2048, 3072], P('ctx', 'head')
- value_grad: bfloat16 [2048, 3072], P('ctx', 'head')
The draws below stay inside these ranges and needn't reach their ends.
Inputs may be any that keep to these rules, and one draw needn't show every extreme that they name: `doc_lengths`: the 16 lengths sum to 2048; the longest is exactly 512.
All inputs are finite; a program needn't handle non-finite values.
Results may differ from the reference program's by a relative error of at most 0.01.
Values sent between devices are 32-bit elements; how exact they have to be, the bound alone decides.
No kernel may reach another device: no remote copies, remote signals or barrier semaphores. Data moves between devices by JAX's collectives and lax.ppermute only.
A program may use at most 256 MiB of HBM per device.

```python
import math
import jax
import jax.numpy as jnp
import numpy as np
from jax import lax

HEAD_TOTAL = 32
HEAD_DIM = 96
TOK_DEV = 128
NDOCS = 16
TOKEN_TOTAL = 2048
FEAT = 3072
MOST_DOC = 512


def draw_values(key, part):
    head_key, noise_key = jax.random.split(jax.random.fold_in(key, 11))
    position = jnp.arange(HEAD_TOTAL, dtype=jnp.float32) / HEAD_TOTAL
    jitter = jax.random.uniform(head_key, (HEAD_TOTAL,), minval=0.8, maxval=1.25)
    ramp = jnp.exp(math.log(0.4) + position * math.log(10.0))
    base = jnp.clip(jax.random.normal(noise_key, (TOKEN_TOTAL, HEAD_TOTAL, HEAD_DIM)), -6.0, 6.0)
    scaled = base * (ramp * jitter)[None, :, None]
    return scaled.reshape(TOKEN_TOTAL, HEAD_TOTAL * HEAD_DIM).astype(jnp.bfloat16)


def draw_decay_log(key, part):
    segment_keys = jax.random.split(jax.random.fold_in(key, 23), 7)
    fast_share = 0.5
    fast = jax.random.uniform(segment_keys[0], (HEAD_TOTAL,)) < fast_share
    fast_rate = jnp.exp(jax.random.uniform(segment_keys[1], (HEAD_TOTAL,), minval=math.log(1.0 / 50.0), maxval=math.log(1.0 / 30.0)))
    slow_rate = math.log(10.0) / TOKEN_TOTAL * jax.random.uniform(segment_keys[2], (HEAD_TOTAL,), minval=0.05, maxval=0.4)
    base_rate = jnp.where(fast, fast_rate, slow_rate)
    blocks = TOKEN_TOTAL // TOK_DEV
    block_factor = jnp.exp(jax.random.uniform(segment_keys[3], (HEAD_TOTAL, blocks), minval=math.log(0.5), maxval=math.log(2.0)))
    rough = jax.random.uniform(segment_keys[4], (HEAD_TOTAL, TOKEN_TOTAL), minval=0.5, maxval=1.5)
    token_wise = base_rate[:, None] * jnp.repeat(block_factor, TOK_DEV, axis=1) * rough
    sudden_spike = jax.random.uniform(segment_keys[5], (TOKEN_TOTAL,)) < 4.0 / TOKEN_TOTAL
    spike_penalty = jax.random.uniform(segment_keys[6], (HEAD_TOTAL, TOKEN_TOTAL), minval=0.2, maxval=0.5)
    spike_logits = jnp.where(sudden_spike[None, :], jnp.log(1.0 - spike_penalty), 0.0)
    return (spike_logits - token_wise).astype(jnp.float32)


def block_scale(stream_key, extent, cuts, smallest, high):
    factor_of, own = 1.0, jax.random.fold_in(stream_key, 6)
    for dim, blocks in cuts:
        heights = jnp.exp(jax.random.uniform(jax.random.fold_in(own, dim), (blocks,), jnp.float32, smallest / len(cuts), high / len(cuts)))
        factor_of = factor_of * jnp.repeat(heights, extent[dim] // blocks).reshape([-1 if axis == dim else 1 for axis in range(len(extent))])
    return factor_of


def length_profile(number_of, total, reach, skew):
    weights = [(1 << 20) // math.isqrt(grade ** skew) + 1 for grade in range(2, number_of + 1)]
    surplus, holding = total - reach - (number_of - 1), [1] * (number_of - 1)
    while surplus > 0:
        free = [i for i in range(number_of - 1) if holding[i] < reach]
        whole, remaining = sum([weights[i] for i in free]), surplus
        for i in free:
            more = min(reach - holding[i], max(1, remaining * weights[i] // whole), surplus)
            holding[i] = holding[i] + more
            surplus = surplus - more
    return np.array([reach] + holding)


def ragged_sizes(stream_key, count, total, reach, skew):
    if count == 2:
        one = jax.random.randint(stream_key, (), max(1, total - reach), min(reach, total - 1) + 1)
        return jnp.stack([one, total - one])
    lengths = jnp.asarray(length_profile(count, total, reach, skew), jnp.int32)
    pairs = (count - 1) // 2
    giver, receiver = lengths[1:1 + 2 * pairs:2], lengths[2:2 + 2 * pairs:2]
    room = jnp.minimum(giver - 1, reach - receiver)
    passed = jax.random.randint(jax.random.fold_in(stream_key, 1), (pairs,), 0, 1 << 20) % (room + 1)
    lengths = lengths.at[1:1 + 2 * pairs:2].set(giver - passed).at[2:2 + 2 * pairs:2].set(receiver + passed)
    return lengths[jax.random.permutation(jax.random.fold_in(stream_key, 2), count)]


def gaussian(own_key, extent, spread, reach, shards=(), held_as=jnp.bfloat16):
    result = spread * jax.random.normal(own_key, extent, jnp.float32)
    if shards:
        result = result * block_scale(own_key, extent, shards, -0.22, 0.18)
    return jnp.clip(result, -reach, reach).astype(held_as)


def setup_inputs(seed: int = 0) -> dict:
    seeds = jax.random.split(jax.random.key(seed), 8)
    queries = gaussian(seeds[0], (TOKEN_TOTAL, FEAT), 1.0, 6.0, ((0, 16), (1, 2)))
    keys = gaussian(seeds[1], (TOKEN_TOTAL, FEAT), 1.0, 6.0, ((0, 16), (1, 2)))
    values = draw_values(jax.random.fold_in(seeds[7], 71), 0)
    decay_log = draw_decay_log(jax.random.fold_in(seeds[7], 71), 0)
    norm_gain = jnp.clip(1.0 + 0.15 * jax.random.normal(seeds[4], (FEAT,), jnp.float32), 0.25, 1.75)
    out_grad = gaussian(seeds[5], (TOKEN_TOTAL, FEAT), 1.0, 6.0, ((0, 16), (1, 2)))
    doc_lengths = ragged_sizes(seeds[6], NDOCS, TOKEN_TOTAL, MOST_DOC, 2).astype(jnp.int32)
    return dict(queries=queries, keys=keys, values=values, decay_log=decay_log, norm_gain=norm_gain, out_grad=out_grad, doc_lengths=doc_lengths)


HIGHEST = lax.Precision.HIGHEST
EPSILON = 1e-06

def doc_starts(doc_lengths):
    doc_ends = jnp.cumsum(doc_lengths).astype(jnp.int32)
    return (doc_ends - doc_lengths).astype(jnp.int32)

def geometry(decay_block, block_start, starts_doc):
    row_count = decay_block.shape[1]
    positions = (block_start + jnp.arange(row_count, dtype=jnp.int32)).astype(jnp.int32)
    doc_index = lax.optimization_barrier(jnp.sum((starts_doc[None, :] <= positions[:, None]).astype(jnp.int32), axis=1))
    doc_before = jnp.sum((starts_doc <= block_start - 1).astype(jnp.int32))
    carry_mask = (doc_index == doc_before).astype(decay_block.dtype)
    log_cum = jnp.cumsum(decay_block, axis=1)
    causal = positions[:, None] >= positions[None, :]
    same_doc = jnp.logical_and(causal, doc_index[:, None] == doc_index[None, :])
    log_gap = jnp.where(same_doc[None], log_cum[:, :, None] - log_cum[:, None, :], 0.0)
    decay_mask = jnp.exp(log_gap) * same_doc[None].astype(decay_block.dtype)
    keep_last = (doc_index == doc_index[row_count - 1]).astype(decay_block.dtype)
    exit_weight = jnp.exp(log_cum[:, row_count - 1:row_count] - log_cum) * keep_last[None, :]
    reach_in = carry_mask[None, :] * jnp.exp(log_cum)
    factor = reach_in[:, row_count - 1]
    return (decay_mask, exit_weight, reach_in, factor)

def rounded(array):
    return lax.optimization_barrier(array.astype(jnp.bfloat16)).astype(jnp.float32)

def reference(queries, keys, values, decay_log, norm_gain, out_grad, doc_lengths):
    head_count, seq_total = decay_log.shape
    feature_count = queries.shape[1]
    head_width = feature_count // head_count
    blocks = seq_total // TOK_DEV
    score_scale = 1.0 / math.sqrt(head_width)
    starts_doc = doc_starts(doc_lengths)

    def split(array):
        return array.reshape(blocks, TOK_DEV, head_count, head_width)
    query_blocks = split(queries)
    key_blocks = split(keys)
    value_blocks = split(values)
    grad_blocks = split(out_grad)
    decay_blocks = decay_log.reshape(head_count, blocks, TOK_DEV).transpose(1, 0, 2)
    block_starts = (jnp.arange(blocks, dtype=jnp.int32) * TOK_DEV).astype(jnp.int32)

    def exit_part(inputs):
        key_block, value_block, decay_block, block_start = inputs
        decay_mask, exit_weight, reach_in, factor = geometry(decay_block, block_start, starts_doc)
        key_f = key_block.astype(jnp.float32)
        value_f = value_block.astype(jnp.float32)
        block_state = jnp.einsum('shd,she->hde', key_f * exit_weight.T[:, :, None], value_f, precision=HIGHEST)
        return (factor, block_state)
    factors, states = lax.map(exit_part, (key_blocks, value_blocks, decay_blocks, block_starts))
    zero_state = jnp.zeros((head_count, head_width, head_width), jnp.float32)

    def chain_step(held, inputs):
        factor, block_state = inputs
        return (factor[:, None, None] * held + block_state, held)
    final_state, incoming = lax.scan(chain_step, zero_state, (factors, states))

    def middle(inputs):
        query_block, key_block, value_block, grad_block, decay_block, block_start, incoming_block = inputs
        decay_mask, exit_weight, reach_in, factor = geometry(decay_block, block_start, starts_doc)
        query_f = query_block.astype(jnp.float32)
        key_f = key_block.astype(jnp.float32)
        value_f = value_block.astype(jnp.float32)
        scores = jnp.einsum('thd,shd->hts', query_f, key_f, precision=HIGHEST)
        attn_probs = rounded(scores * score_scale * decay_mask)
        local_part = jnp.einsum('hts,shd->thd', attn_probs, value_f, precision=HIGHEST)
        carried = jnp.einsum('thd,hde->the', query_f, incoming_block, precision=HIGHEST)
        attended = (local_part + score_scale * reach_in.T[:, :, None] * carried).reshape(TOK_DEV, feature_count)
        inv_rms = lax.rsqrt(lax.optimization_barrier(jnp.sum(attended * attended, axis=1)) / feature_count + EPSILON)
        output_block = (attended * inv_rms[:, None] * norm_gain[None, :]).astype(jnp.bfloat16)
        grad_gain = grad_block.reshape(TOK_DEV, feature_count).astype(jnp.float32) * norm_gain[None, :]
        grad_dot = lax.optimization_barrier(jnp.sum(grad_gain * attended, axis=1))
        attended_grad = (grad_gain * inv_rms[:, None] - attended * (inv_rms ** 3 * grad_dot / feature_count)[:, None]).astype(jnp.bfloat16)
        grad_f = attended_grad.reshape(TOK_DEV, head_count, head_width).astype(jnp.float32)
        block_grad = score_scale * jnp.einsum('thd,the->hde', query_f * reach_in.T[:, :, None], grad_f, precision=HIGHEST)
        return (output_block, attended_grad, block_grad)
    outputs, attended_grads, block_grads = lax.map(middle, (query_blocks, key_blocks, value_blocks, grad_blocks, decay_blocks, block_starts, incoming))
    final_grad, later = lax.scan(chain_step, zero_state, (factors, block_grads), reverse=True)

    def finish(inputs):
        query_block, key_block, value_block, attended_grad, decay_block, block_start, incoming_block, later_block = inputs
        decay_mask, exit_weight, reach_in, factor = geometry(decay_block, block_start, starts_doc)
        query_f = query_block.astype(jnp.float32)
        key_f = key_block.astype(jnp.float32)
        value_f = value_block.astype(jnp.float32)
        grad_f = attended_grad.reshape(TOK_DEV, head_count, head_width).astype(jnp.float32)
        scores = jnp.einsum('thd,shd->hts', query_f, key_f, precision=HIGHEST)
        attn_probs = rounded(scores * score_scale * decay_mask)
        grad_scores = jnp.einsum('thd,shd->hts', grad_f, value_f, precision=HIGHEST)
        score_grad = rounded(grad_scores * score_scale * decay_mask)
        query_part = jnp.einsum('hts,shd->thd', score_grad, key_f, precision=HIGHEST)
        query_part = query_part + score_scale * reach_in.T[:, :, None] * jnp.einsum('the,hde->thd', grad_f, incoming_block, precision=HIGHEST)
        key_part = jnp.einsum('hts,thd->shd', score_grad, query_f, precision=HIGHEST)
        key_part = key_part + exit_weight.T[:, :, None] * jnp.einsum('she,hde->shd', value_f, later_block, precision=HIGHEST)
        value_part = jnp.einsum('hts,the->she', attn_probs, grad_f, precision=HIGHEST)
        value_part = value_part + exit_weight.T[:, :, None] * jnp.einsum('shd,hde->she', key_f, later_block, precision=HIGHEST)
        return (query_part.reshape(TOK_DEV, feature_count).astype(jnp.bfloat16), key_part.reshape(TOK_DEV, feature_count).astype(jnp.bfloat16), value_part.reshape(TOK_DEV, feature_count).astype(jnp.bfloat16))
    query_grads, key_grads, value_grads = lax.map(finish, (query_blocks, key_blocks, value_blocks, attended_grads, decay_blocks, block_starts, incoming, later))
    return (outputs.reshape(seq_total, feature_count), query_grads.reshape(seq_total, feature_count), key_grads.reshape(seq_total, feature_count), value_grads.reshape(seq_total, feature_count))
```

```python
import functools
import math

import jax
import jax.numpy as jnp
from jax import lax
from jax.experimental import pallas as pl
from jax.experimental.pallas import tpu as pltpu
from jax.sharding import PartitionSpec as P

EPSILON = 1e-06
NEVER = -1e30
F32 = jnp.float32
BF16 = jnp.bfloat16
NN = (((1,), (0,)), ((), ()))
NT = (((1,), (1,)), ((), ()))
TN = (((0,), (0,)), ((), ()))


def dot(a, b, dims=NN):
    return lax.dot_general(a, b, dims, preferred_element_type=F32)


def split3(x):
    a = x.astype(BF16)
    rest = x - a.astype(F32)
    b = rest.astype(BF16)
    return a, b, (rest - b.astype(F32)).astype(BF16)


def exact_dot(x, ones, dims, x_first):
    out = None
    for part in split3(x):
        term = dot(part, ones, dims) if x_first else dot(ones, part, dims)
        out = term if out is None else out + term
    return out


class Plan:
    def __init__(self, tokens, width, heads, pieces):
        self.tokens, self.width, self.heads = tokens, width, heads
        self.dim = width // heads
        self.group = math.lcm(self.dim, 128) // self.dim
        self.lanes = self.group * self.dim
        self.groups = heads // self.group
        self.pieces = pieces
        self.rows = self.dim // pieces
        self.tiles = width // 128
        self.scale = 1.0 / math.sqrt(self.dim)
        self.piece_rows = self.tiles * self.rows
        self.factor_rows = -(-self.tiles // 8) * 8


def iota(shape, dim):
    return lax.broadcasted_iota(jnp.int32, shape, dim)


def tri(n, keep):
    return keep(iota((n, n), 0), iota((n, n), 1)).astype(F32).astype(BF16)


def head_mask(plan, k):
    lane = iota((1, plan.lanes), 1)
    return (lane >= k * plan.dim) & (lane < (k + 1) * plan.dim)


def spread(plan, columns):
    head, lane = iota((plan.heads, plan.width), 0), iota((plan.heads, plan.width), 1)
    ones = ((lane >= head * plan.dim) & (lane < (head + 1) * plan.dim)).astype(F32).astype(BF16)
    high = columns.astype(BF16)
    low = (columns - high.astype(F32)).astype(BF16)
    return dot(high, ones) + dot(low, ones)


def doc_edges(plan, lengths_ref, block_start):
    start = jnp.int32(0)
    last, first = jnp.int32(0), jnp.int32(2**30)
    for i in range(lengths_ref.shape[0]):
        last = jnp.where(start < block_start + plan.tokens, start, last)
        first = jnp.where(start >= block_start, jnp.minimum(first, start), first)
        start = start + lengths_ref[i]
    return last, first


def doc_index(lengths_ref, positions):
    start = jnp.int32(0)
    index = jnp.zeros(positions.shape, jnp.int32)
    for i in range(lengths_ref.shape[0]):
        index = index + (positions >= start).astype(jnp.int32)
        start = start + lengths_ref[i]
    return index


def exit_columns(plan, decay, last, block_start):
    after = tri(plan.tokens, lambda t, u: u > t)
    keep = block_start + iota((plan.tokens, plan.heads), 0) >= last
    return jnp.where(keep, jnp.exp(exact_dot(decay, after, NT, False)), 0.0)


def reach_columns(plan, decay, first, block_start):
    until = tri(plan.tokens, lambda t, u: u <= t)
    carry = block_start + iota((plan.tokens, plan.heads), 0) < first
    return jnp.where(carry, jnp.exp(exact_dot(decay, until, NT, False)), 0.0)


def decay_bias(plan, lengths_ref, block_start):
    n = plan.tokens
    t, s = iota((n, n), 0), iota((n, n), 1)
    same = doc_index(lengths_ref, t + block_start) == doc_index(lengths_ref, s + block_start)
    return jnp.where(same & (t >= s), math.log(plan.scale), NEVER)


def log_sums(plan, decay):
    until = tri(plan.tokens, lambda t, u: u <= t)
    return exact_dot(decay, until, NT, False), exact_dot(decay, until, NT, True)


def own_heads(plan, product, rows):
    out = product[:rows]
    for k in range(1, plan.group):
        out = jnp.where(head_mask(plan, k), product[k * rows : (k + 1) * rows], out)
    return out


def stack_heads(plan, x):
    return jnp.concatenate(
        [jnp.where(head_mask(plan, k), x, jnp.zeros_like(x)) for k in range(plan.group)], axis=0
    )


def lanes_of(plan, g):
    return slice(g * plan.lanes, (g + 1) * plan.lanes)


def store_pieces(plan, mine, state_ref, piece_refs):
    for m, piece in enumerate(piece_refs):
        start = pl.multiple_of((mine ^ m) * plan.rows, plan.rows)
        for j in range(plan.tiles):
            piece[j * plan.rows : (j + 1) * plan.rows, :] = state_ref[
                pl.ds(start, plan.rows), j * 128 : (j + 1) * 128
            ]


def load_pieces(plan, mine, piece_refs, state_ref):
    for m, piece in enumerate(piece_refs):
        start = pl.multiple_of((mine ^ m) * plan.rows, plan.rows)
        for j in range(plan.tiles):
            state_ref[pl.ds(start, plan.rows), j * 128 : (j + 1) * 128] = piece[
                j * plan.rows : (j + 1) * plan.rows, :
            ]


def exit_kernel(plan, place_ref, lengths_ref, decay_ref, keys_ref, values_ref, *refs):
    pieces, (weighted_ref, state_ref) = refs[: plan.pieces], refs[plan.pieces :]
    block_start, mine = place_ref[0], place_ref[1]
    last, first = doc_edges(plan, lengths_ref, block_start)
    decay = decay_ref[...]
    weights = spread(plan, exit_columns(plan, decay, last, block_start))
    for g in range(plan.groups):
        at = lanes_of(plan, g)
        weighted = (keys_ref[:, at].astype(F32) * weights[:, at]).astype(BF16)
        weighted_ref[:, at] = weighted
        state_ref[:, at] = own_heads(plan, dot(weighted, values_ref[:, at], TN), plan.dim)
    store_pieces(plan, mine, state_ref, pieces)
    whole = jnp.exp(jnp.sum(decay, axis=1, keepdims=True))
    whole = jnp.where(first >= block_start + plan.tokens, whole, 0.0)
    head = iota((plan.heads, 128), 0)
    rows = []
    for j in range(plan.tiles):
        lane = iota((plan.heads, 128), 1) + j * 128
        on = (lane >= head * plan.dim) & (lane < (head + 1) * plan.dim)
        rows.append(jnp.sum(jnp.where(on, whole, 0.0), axis=0, keepdims=True))
    rows.append(jnp.zeros((plan.factor_rows - plan.tiles, 128), F32))
    rows = jnp.concatenate(rows, axis=0)
    for piece in pieces:
        piece[plan.piece_rows :, :] = rows


def chain_kernel(plan, reverse, with_carry, place_ref, *refs):
    n = plan.pieces
    pieces, factors = refs[:n], refs[n : 2 * n]
    mine = place_ref[1]
    rows = plan.rows
    order = range(n - 1, -1, -1) if reverse else range(n)
    slot = [mine ^ j for j in range(n)]
    state_scratch, factor_scratch = refs[-2], refs[-1]
    for m in range(n):
        state_scratch[mine ^ m] = pieces[m][: plan.piece_rows, :]
        factor_scratch[mine ^ m] = factors[m][-plan.factor_rows :, :]
    if with_carry:
        held = refs[2 * n][...]
        outs_ref = refs[-3]
    else:
        held = jnp.zeros((plan.piece_rows, 128), F32)
        outs_ref = None
    tiles = [held[j * rows : (j + 1) * rows] for j in range(plan.tiles)]
    for step, b in enumerate(order):
        if with_carry:
            for j in range(plan.tiles):
                outs_ref[b, j * rows : (j + 1) * rows, :] = tiles[j]
            if step == n - 1:
                break
        for j in range(plan.tiles):
            tiles[j] = (
                tiles[j] * factor_scratch[b, j : j + 1, :]
                + state_scratch[b, j * rows : (j + 1) * rows, :]
            )
    if with_carry:
        outs = refs[2 * n + 1 : 3 * n + 1]
        for m in range(n):
            outs[m][...] = outs_ref[mine ^ m]
    else:
        for j in range(plan.tiles):
            refs[2 * n][j * rows : (j + 1) * rows, :] = tiles[j]


def local_kernel(
    plan, place_ref, lengths_ref, decay_ref, queries_ref, keys_ref, values_ref, probs_ref, local_ref, reached_ref
):
    block_start = place_ref[0]
    decay = decay_ref[...]
    last, first = doc_edges(plan, lengths_ref, block_start)
    columns, rows = log_sums(plan, decay)
    bias = decay_bias(plan, lengths_ref, block_start)
    carry = block_start + iota(columns.shape, 0) < first
    reach = spread(plan, jnp.where(carry, jnp.exp(columns), 0.0) * plan.scale)
    n = plan.tokens
    for g in range(plan.groups):
        at = lanes_of(plan, g)
        queries, keys, values = queries_ref[:, at], keys_ref[:, at], values_ref[:, at]
        reached_ref[:, at] = (queries.astype(F32) * reach[:, at]).astype(BF16)
        scores = dot(stack_heads(plan, queries), keys, NT)
        probs = []
        for k in range(plan.group):
            h = g * plan.group + k
            mask = jnp.exp(columns[:, h : h + 1] - rows[h : h + 1, :] + bias)
            probs.append((scores[k * n : (k + 1) * n] * mask).astype(BF16))
        probs = jnp.concatenate(probs, axis=1)
        probs_ref[:, g * plan.group * n : (g + 1) * plan.group * n] = probs
        local_ref[:, at] = dot(probs, stack_heads(plan, values))


def attend_kernel(plan, place_ref, local_ref, reached_ref, out_grad_ref, gain_ref, *refs):
    pieces = refs[: plan.pieces]
    attended_ref, sums_ref, incoming_ref, state_ref = refs[plan.pieces :]
    load_pieces(plan, place_ref[1], pieces, state_ref)
    squares = inner = None
    for g in range(plan.groups):
        at = lanes_of(plan, g)
        incoming = state_ref[:, at].astype(BF16)
        incoming_ref[:, at] = incoming
        attended = local_ref[:, at] + dot(reached_ref[:, at], stack_heads(plan, incoming))
        attended_ref[:, at] = attended
        grad = out_grad_ref[:, at].astype(F32) * gain_ref[:, at]
        square, product = attended * attended, grad * attended
        for j in range(0, plan.lanes, 128):
            squares = square[:, j : j + 128] if squares is None else squares + square[:, j : j + 128]
            inner = product[:, j : j + 128] if inner is None else inner + product[:, j : j + 128]
    lane = iota((plan.tokens, 128), 1)
    sums_ref[...] = jnp.where(
        lane < 64, jnp.sum(squares, axis=1, keepdims=True), jnp.sum(inner, axis=1, keepdims=True)
    )


def grad_kernel(
    plan, features, place_ref, attended_ref, out_grad_ref, gain_ref, sums_ref, other_ref, reached_ref, *refs
):
    pieces, (attended_grad_ref, norm_ref, state_ref) = refs[: plan.pieces], refs[plan.pieces :]
    sums = sums_ref[...] + other_ref[...]
    inverse = lax.rsqrt(sums[:, :1] / features + EPSILON)
    norm_ref[...] = jnp.broadcast_to(inverse, norm_ref.shape)
    slope = inverse * inverse * inverse * sums[:, 64:65] / features
    for g in range(plan.groups):
        at = lanes_of(plan, g)
        grad = out_grad_ref[:, at].astype(F32) * gain_ref[:, at]
        attended_grad = (grad * inverse - attended_ref[:, at] * slope).astype(BF16)
        attended_grad_ref[:, at] = attended_grad
        state_ref[:, at] = own_heads(plan, dot(reached_ref[:, at], attended_grad, TN), plan.dim)
    store_pieces(plan, place_ref[1], state_ref, pieces)


def inner_kernel(
    plan,
    place_ref,
    lengths_ref,
    decay_ref,
    queries_ref,
    keys_ref,
    values_ref,
    gain_ref,
    attended_ref,
    attended_grad_ref,
    norm_ref,
    probs_ref,
    incoming_ref,
    output_ref,
    query_grad_ref,
    key_local_ref,
    value_local_ref,
    weighted_ref,
):
    block_start = place_ref[0]
    decay = decay_ref[...]
    last, first = doc_edges(plan, lengths_ref, block_start)
    columns, rows = log_sums(plan, decay)
    bias = decay_bias(plan, lengths_ref, block_start)
    position = block_start + iota(columns.shape, 0)
    reach = spread(plan, jnp.where(position < first, jnp.exp(columns), 0.0) * plan.scale)
    exits = spread(plan, exit_columns(plan, decay, last, block_start))
    norm = norm_ref[:, :1]
    n = plan.tokens
    for g in range(plan.groups):
        at = lanes_of(plan, g)
        output_ref[:, at] = (attended_ref[:, at] * norm * gain_ref[:, at]).astype(BF16)
        queries, keys, values = queries_ref[:, at], keys_ref[:, at], values_ref[:, at]
        grads = attended_grad_ref[:, at]
        weighted_ref[:, at] = (values.astype(F32) * exits[:, at]).astype(BF16)
        scores = dot(stack_heads(plan, grads), values, NT)
        score_grads = []
        for k in range(plan.group):
            h = g * plan.group + k
            mask = jnp.exp(columns[:, h : h + 1] - rows[h : h + 1, :] + bias)
            score_grads.append((scores[k * n : (k + 1) * n] * mask).astype(BF16))
        score_grads = jnp.concatenate(score_grads, axis=1)
        probs = probs_ref[:, g * plan.group * n : (g + 1) * plan.group * n]
        query_grad = dot(score_grads, stack_heads(plan, keys))
        query_grad += reach[:, at] * dot(grads, stack_heads(plan, incoming_ref[:, at]), NT)
        query_grad_ref[:, at] = query_grad.astype(BF16)
        key_local_ref[:, at] = own_heads(plan, dot(score_grads, queries, TN), n)
        value_local_ref[:, at] = own_heads(plan, dot(probs, grads, TN), n)


def finish_kernel(
    plan, place_ref, key_local_ref, value_local_ref, weighted_values_ref, weighted_keys_ref, *refs
):
    pieces, (key_grad_ref, value_grad_ref, state_ref) = refs[: plan.pieces], refs[plan.pieces :]
    load_pieces(plan, place_ref[1], pieces, state_ref)
    for g in range(plan.groups):
        at = lanes_of(plan, g)
        later = stack_heads(plan, state_ref[:, at].astype(BF16))
        key_grad = key_local_ref[:, at] + dot(weighted_values_ref[:, at], later, NT)
        key_grad_ref[:, at] = key_grad.astype(BF16)
        value_grad = value_local_ref[:, at] + dot(weighted_keys_ref[:, at], later)
        value_grad_ref[:, at] = value_grad.astype(BF16)


SCALAR = pl.BlockSpec(memory_space=pltpu.SMEM)
WHOLE = pl.BlockSpec(memory_space=pltpu.VMEM)


def call(kernel, name, scalars, arrays, outs, scratch=(), flops=0):
    moved = sum(a.size * a.dtype.itemsize for a in (*arrays, *outs))
    return pl.pallas_call(
        kernel,
        name=name,
        out_shape=outs,
        in_specs=[SCALAR] * len(scalars) + [WHOLE] * len(arrays),
        out_specs=[WHOLE] * len(outs),
        scratch_shapes=list(scratch),
        compiler_params=pltpu.CompilerParams(vmem_limit_bytes=40 * 2**20),
        cost_estimate=pl.CostEstimate(flops=flops, bytes_accessed=moved, transcendentals=0),
    )(*scalars, *arrays)


def array(*shape, dtype=F32):
    return jax.ShapeDtypeStruct(shape, dtype)


def exchange(pieces, count):
    return [pieces[0]] + [
        lax.ppermute(piece, "ctx", [(i, i ^ m) for i in range(count)])
        for m, piece in enumerate(pieces)
        if m
    ]


def shift(x, count, by):
    pairs = [(i, i + by) for i in range(count) if 0 <= i + by < count]
    return lax.ppermute(x, "ctx", pairs)


def scan_whole(plan, state, factor, count, reach, sign):
    held = shift(state, count, sign)
    rates = shift(factor, count, sign)
    by = 1
    while by < reach:
        held = held + rates * shift(held, count, sign * by)
        rates = rates * shift(rates, count, sign * by)
        by *= 2
    return held


def on_device(queries, keys, values, decay_log, norm_gain, out_grad, doc_lengths):
    tokens, width = queries.shape
    heads = decay_log.shape[0]
    count = lax.axis_size("ctx")
    features = width * lax.axis_size("head")
    reach = count // 4
    even = reach & (reach - 1) == 0 and (width // heads) % (8 * reach) == 0
    plan = Plan(tokens, width, heads, reach if even else 1)
    n = plan.pieces
    index = lax.axis_index("ctx")
    place = jnp.stack([index * tokens, index % n]).astype(jnp.int32)
    gain = norm_gain.reshape(1, width)
    like = array(tokens, width, dtype=BF16)
    wide = array(tokens, width)
    state = pltpu.VMEM((plan.dim, width), F32)
    piece = array(plan.piece_rows, 128)
    framed = array(plan.piece_rows + plan.factor_rows, 128)

    *pieces, weighted_keys = call(
        functools.partial(exit_kernel, plan),
        "exit_states",
        (place, doc_lengths),
        (decay_log, keys, values),
        [framed] * n + [like],
        [state],
        flops=10**8,
    )
    if even:
        pieces = exchange(pieces, count)
    frames = pieces

    def chain(pieces, reverse, carry=None):
        with_carry = carry is not None
        scratch = [pltpu.VMEM((n, plan.piece_rows, 128), F32), pltpu.VMEM((n, plan.factor_rows, 128), F32)]
        if with_carry:
            scratch = [pltpu.VMEM((n, plan.piece_rows, 128), F32)] + scratch
        return call(
            functools.partial(chain_kernel, plan, reverse, with_carry),
            "prefix_states" if with_carry else "total_state",
            (place,),
            (*pieces, *frames, carry) if with_carry else (*pieces, *frames),
            [piece] * n if with_carry else [piece],
            scratch,
        )

    def entering(pieces, reverse):
        sign = -1 if reverse else 1
        if not even:
            whole = pieces[0][: plan.piece_rows].reshape(plan.tiles, plan.rows, 128)
            factor = frames[0][plan.piece_rows : plan.piece_rows + plan.tiles, None, :]
            return [scan_whole(plan, whole, factor, count, reach, sign).reshape(piece.shape)]
        (total,) = chain(pieces, reverse)
        carry = shift(total, count, sign * n)
        return exchange(chain(pieces, reverse, carry), count)

    incoming = entering(pieces, False)
    probs, local, reached = call(
        functools.partial(local_kernel, plan),
        "local_attention",
        (place, doc_lengths),
        (decay_log, queries, keys, values),
        [array(tokens, heads * tokens, dtype=BF16), wide, like],
        flops=10**9,
    )
    attended, sums, incoming_state = call(
        functools.partial(attend_kernel, plan),
        "attended",
        (place,),
        (local, reached, out_grad, gain, *incoming),
        [wide, array(tokens, 128), array(plan.dim, width, dtype=BF16)],
        [state],
    )
    other = lax.ppermute(sums, "head", [(0, 1), (1, 0)])
    *pieces, attended_grad, norm = call(
        functools.partial(grad_kernel, plan, features),
        "attended_grad",
        (place,),
        (attended, out_grad, gain, sums, other, reached),
        [piece] * n + [like, array(tokens, 128)],
        [state],
    )
    if even:
        pieces = exchange(pieces, count)
    later = entering(pieces, True)
    output, query_grad, key_local, value_local, weighted_values = call(
        functools.partial(inner_kernel, plan),
        "local_grads",
        (place, doc_lengths),
        (
            decay_log,
            queries,
            keys,
            values,
            gain,
            attended,
            attended_grad,
            norm,
            probs,
            incoming_state,
        ),
        [like, like, wide, wide, like],
        flops=10**9,
    )
    key_grad, value_grad = call(
        functools.partial(finish_kernel, plan),
        "key_value_grads",
        (place,),
        (key_local, value_local, weighted_values, weighted_keys, *later),
        [like, like],
        [state],
    )
    return (output, query_grad, key_grad, value_grad)


def solution(mesh):
    in_specs = (
        P("ctx", "head"),
        P("ctx", "head"),
        P("ctx", "head"),
        P("head", "ctx"),
        P("head"),
        P("ctx", "head"),
        P(),
    )
    out_specs = (P("ctx", "head"), P("ctx", "head"), P("ctx", "head"), P("ctx", "head"))
    return jax.shard_map(
        on_device, mesh=mesh, in_specs=in_specs, out_specs=out_specs, check_vma=False
    )
```

```python
import functools
import math

import jax
import jax.numpy as jnp
from jax import lax
from jax.experimental import pallas as pl
from jax.experimental.pallas import tpu as pltpu
from jax.sharding import PartitionSpec as P

EPSILON = 1e-06
NEVER = -1e30
F32 = jnp.float32
BF16 = jnp.bfloat16
NN = (((1,), (0,)), ((), ()))
NT = (((1,), (1,)), ((), ()))
TN = (((0,), (0,)), ((), ()))


def dot(a, b, dims=NN):
    return lax.dot_general(a, b, dims, preferred_element_type=F32)


def split3(x):
    a = x.astype(BF16)
    rest = x - a.astype(F32)
    b = rest.astype(BF16)
    return a, b, (rest - b.astype(F32)).astype(BF16)


def exact_dot(x, ones, dims, x_first):
    out = None
    for part in split3(x):
        term = dot(part, ones, dims) if x_first else dot(ones, part, dims)
        out = term if out is None else out + term
    return out


class Plan:
    def __init__(self, tokens, width, heads, pieces):
        self.tokens, self.width, self.heads = tokens, width, heads
        self.dim = width // heads
        self.group = math.lcm(self.dim, 128) // self.dim
        self.lanes = self.group * self.dim
        self.groups = heads // self.group
        self.pieces = pieces
        self.rows = self.dim // pieces
        self.tiles = width // 128
        self.scale = 1.0 / math.sqrt(self.dim)
        self.piece_rows = self.tiles * self.rows
        self.factor_rows = -(-self.tiles // 8) * 8


def place(plan):
    index = lax.axis_index("ctx")
    return index * plan.tokens, lax.rem(index, plan.pieces)


def iota(shape, dim):
    return lax.broadcasted_iota(jnp.int32, shape, dim)


def tri(n, keep):
    return keep(iota((n, n), 0), iota((n, n), 1)).astype(F32).astype(BF16)


def head_mask(plan, k):
    lane = iota((1, plan.lanes), 1)
    return (lane >= k * plan.dim) & (lane < (k + 1) * plan.dim)


def spread(plan, columns):
    head, lane = iota((plan.heads, plan.width), 0), iota((plan.heads, plan.width), 1)
    ones = ((lane >= head * plan.dim) & (lane < (head + 1) * plan.dim)).astype(F32).astype(BF16)
    high = columns.astype(BF16)
    low = (columns - high.astype(F32)).astype(BF16)
    return dot(high, ones) + dot(low, ones)


def doc_edges(plan, lengths_ref, block_start):
    start = jnp.int32(0)
    last, first = jnp.int32(0), jnp.int32(2**30)
    for i in range(lengths_ref.shape[0]):
        last = jnp.where(start < block_start + plan.tokens, start, last)
        first = jnp.where(start >= block_start, jnp.minimum(first, start), first)
        start = start + lengths_ref[i]
    return last, first


def doc_index(lengths_ref, positions):
    start = jnp.int32(0)
    index = jnp.zeros(positions.shape, jnp.int32)
    for i in range(lengths_ref.shape[0]):
        index = index + (positions >= start).astype(jnp.int32)
        start = start + lengths_ref[i]
    return index


def exit_columns(plan, decay, last, block_start):
    after = tri(plan.tokens, lambda t, u: u > t)
    keep = block_start + iota((plan.tokens, plan.heads), 0) >= last
    return jnp.where(keep, jnp.exp(exact_dot(decay, after, NT, False)), 0.0)


def reach_columns(plan, decay, first, block_start):
    until = tri(plan.tokens, lambda t, u: u <= t)
    carry = block_start + iota((plan.tokens, plan.heads), 0) < first
    return jnp.where(carry, jnp.exp(exact_dot(decay, until, NT, False)), 0.0)


def decay_bias(plan, lengths_ref, block_start):
    n = plan.tokens
    t, s = iota((n, n), 0), iota((n, n), 1)
    same = doc_index(lengths_ref, t + block_start) == doc_index(lengths_ref, s + block_start)
    return jnp.where(same & (t >= s), math.log(plan.scale), NEVER)


def log_sums(plan, decay):
    until = tri(plan.tokens, lambda t, u: u <= t)
    return exact_dot(decay, until, NT, False), exact_dot(decay, until, NT, True)


def own_heads(plan, product, rows):
    out = product[:rows]
    for k in range(1, plan.group):
        out = jnp.where(head_mask(plan, k), product[k * rows : (k + 1) * rows], out)
    return out


def stack_heads(plan, x):
    return jnp.concatenate(
        [jnp.where(head_mask(plan, k), x, jnp.zeros_like(x)) for k in range(plan.group)], axis=0
    )


def lanes_of(plan, g):
    return slice(g * plan.lanes, (g + 1) * plan.lanes)


def store_pieces(plan, mine, state_ref, piece_refs):
    for m, piece in enumerate(piece_refs):
        start = pl.multiple_of((mine ^ m) * plan.rows, plan.rows)
        for j in range(plan.tiles):
            piece[j * plan.rows : (j + 1) * plan.rows, :] = state_ref[
                pl.ds(start, plan.rows), j * 128 : (j + 1) * 128
            ]


def load_pieces(plan, mine, piece_refs, state_ref):
    for m, piece in enumerate(piece_refs):
        start = pl.multiple_of((mine ^ m) * plan.rows, plan.rows)
        for j in range(plan.tiles):
            state_ref[pl.ds(start, plan.rows), j * 128 : (j + 1) * 128] = piece[
                j * plan.rows : (j + 1) * plan.rows, :
            ]


def row_copies(source, target, sems):
    count = sems.shape[0]
    rows = source.shape[0] // count
    return [
        pltpu.make_async_copy(
            source.at[i * rows : (i + 1) * rows], target.at[i * rows : (i + 1) * rows], sems.at[i]
        )
        for i in range(count)
    ]


def exit_kernel(plan, lengths_hbm, decay_hbm, keys_hbm, values_hbm, *refs):
    pieces = refs[: plan.pieces]
    weighted_ref, lengths_ref, decay_ref, keys_ref, values_ref, state_ref, small_sems, key_sems, value_sems = refs[
        plan.pieces :
    ]
    lengths_copy = pltpu.make_async_copy(lengths_hbm, lengths_ref, small_sems.at[0])
    decay_copy = pltpu.make_async_copy(decay_hbm, decay_ref, small_sems.at[1])
    lengths_copy.start()
    decay_copy.start()
    keys_copies = row_copies(keys_hbm, keys_ref, key_sems)
    values_copies = row_copies(values_hbm, values_ref, value_sems)
    for copy in keys_copies + values_copies:
        copy.start()
    block_start, mine = place(plan)
    lengths_copy.wait()
    last, first = doc_edges(plan, lengths_ref, block_start)
    decay_copy.wait()
    decay = decay_ref[...]
    weights = spread(plan, exit_columns(plan, decay, last, block_start))
    whole = jnp.exp(jnp.sum(decay, axis=1, keepdims=True))
    whole = jnp.where(first >= block_start + plan.tokens, whole, 0.0)
    head = iota((plan.heads, 128), 0)
    rows = []
    for j in range(plan.tiles):
        lane = iota((plan.heads, 128), 1) + j * 128
        on = (lane >= head * plan.dim) & (lane < (head + 1) * plan.dim)
        rows.append(jnp.sum(jnp.where(on, whole, 0.0), axis=0, keepdims=True))
    rows.append(jnp.zeros((plan.factor_rows - plan.tiles, 128), F32))
    rows = jnp.concatenate(rows, axis=0)
    for piece in pieces:
        piece[plan.piece_rows :, :] = rows
    for copy in keys_copies:
        copy.wait()
    weighted_ref[...] = (keys_ref[...].astype(F32) * weights).astype(BF16)
    for copy in values_copies:
        copy.wait()
    for g in range(plan.groups):
        at = lanes_of(plan, g)
        state_ref[:, at] = own_heads(plan, dot(weighted_ref[:, at], values_ref[:, at], TN), plan.dim)
    store_pieces(plan, mine, state_ref, pieces)


def chain_kernel(plan, reverse, with_carry, *refs):
    n, rows = plan.pieces, plan.rows
    pieces, factors = refs[:n], refs[n : 2 * n]
    carry_ref = refs[2 * n] if with_carry else None
    outs = refs[2 * n + 1 :] if with_carry else refs[2 * n :]
    order = range(n - 1, -1, -1) if reverse else range(n)

    def at_place(mine):
        for j in range(plan.tiles):
            at = slice(j * rows, (j + 1) * rows)
            tile = carry_ref[at] if with_carry else None
            for step, b in enumerate(order):
                m = mine ^ b
                if with_carry:
                    outs[m][at] = tile
                    if step == n - 1:
                        break
                rate = factors[m][plan.piece_rows + j : plan.piece_rows + j + 1, :]
                tile = pieces[m][at] if tile is None else tile * rate + pieces[m][at]
            if not with_carry:
                outs[0][at] = tile

    own = place(plan)[1]
    for mine in range(n):
        pl.when(own == mine)(functools.partial(at_place, mine))


def local_kernel(
    plan, lengths_ref, decay_ref, queries_ref, keys_ref, values_ref, probs_ref, local_ref, reached_ref
):
    block_start = place(plan)[0]
    decay = decay_ref[...]
    last, first = doc_edges(plan, lengths_ref, block_start)
    columns, rows = log_sums(plan, decay)
    bias = decay_bias(plan, lengths_ref, block_start)
    carry = block_start + iota(columns.shape, 0) < first
    reach = spread(plan, jnp.where(carry, jnp.exp(columns), 0.0) * plan.scale)
    n = plan.tokens
    for g in range(plan.groups):
        at = lanes_of(plan, g)
        queries, keys, values = queries_ref[:, at], keys_ref[:, at], values_ref[:, at]
        reached_ref[:, at] = (queries.astype(F32) * reach[:, at]).astype(BF16)
        scores = dot(stack_heads(plan, queries), keys, NT)
        probs = []
        for k in range(plan.group):
            h = g * plan.group + k
            mask = jnp.exp(columns[:, h : h + 1] - rows[h : h + 1, :] + bias)
            probs.append((scores[k * n : (k + 1) * n] * mask).astype(BF16))
        probs = jnp.concatenate(probs, axis=1)
        probs_ref[:, g * plan.group * n : (g + 1) * plan.group * n] = probs
        local_ref[:, at] = dot(probs, stack_heads(plan, values))


def attend_kernel(plan, local_ref, reached_ref, out_grad_ref, gain_ref, *refs):
    pieces = refs[: plan.pieces]
    attended_ref, sums_ref, incoming_ref, state_ref = refs[plan.pieces :]
    load_pieces(plan, place(plan)[1], pieces, state_ref)
    squares = inner = None
    for g in range(plan.groups):
        at = lanes_of(plan, g)
        incoming = state_ref[:, at].astype(BF16)
        incoming_ref[:, at] = incoming
        attended = local_ref[:, at] + dot(reached_ref[:, at], stack_heads(plan, incoming))
        attended_ref[:, at] = attended
        grad = out_grad_ref[:, at].astype(F32) * gain_ref[:, at]
        square, product = attended * attended, grad * attended
        for j in range(0, plan.lanes, 128):
            squares = square[:, j : j + 128] if squares is None else squares + square[:, j : j + 128]
            inner = product[:, j : j + 128] if inner is None else inner + product[:, j : j + 128]
    lane = iota((plan.tokens, 128), 1)
    sums_ref[...] = jnp.where(
        lane < 64, jnp.sum(squares, axis=1, keepdims=True), jnp.sum(inner, axis=1, keepdims=True)
    )


def grad_kernel(
    plan, features, attended_ref, out_grad_ref, gain_ref, sums_ref, other_ref, reached_ref, *refs
):
    pieces, (attended_grad_ref, norm_ref, state_ref) = refs[: plan.pieces], refs[plan.pieces :]
    sums = sums_ref[...] + other_ref[...]
    inverse = lax.rsqrt(sums[:, :1] / features + EPSILON)
    norm_ref[...] = jnp.broadcast_to(inverse, norm_ref.shape)
    slope = inverse * inverse * inverse * sums[:, 64:65] / features
    for g in range(plan.groups):
        at = lanes_of(plan, g)
        grad = out_grad_ref[:, at].astype(F32) * gain_ref[:, at]
        attended_grad = (grad * inverse - attended_ref[:, at] * slope).astype(BF16)
        attended_grad_ref[:, at] = attended_grad
        state_ref[:, at] = own_heads(plan, dot(reached_ref[:, at], attended_grad, TN), plan.dim)
    store_pieces(plan, place(plan)[1], state_ref, pieces)


def inner_kernel(
    plan,
    lengths_ref,
    decay_ref,
    queries_ref,
    keys_ref,
    values_ref,
    gain_ref,
    attended_ref,
    attended_grad_ref,
    norm_ref,
    probs_ref,
    incoming_ref,
    output_ref,
    query_grad_ref,
    key_local_ref,
    value_local_ref,
    weighted_ref,
):
    block_start = place(plan)[0]
    decay = decay_ref[...]
    last, first = doc_edges(plan, lengths_ref, block_start)
    columns, rows = log_sums(plan, decay)
    bias = decay_bias(plan, lengths_ref, block_start)
    position = block_start + iota(columns.shape, 0)
    reach = spread(plan, jnp.where(position < first, jnp.exp(columns), 0.0) * plan.scale)
    exits = spread(plan, exit_columns(plan, decay, last, block_start))
    norm = norm_ref[:, :1]
    n = plan.tokens
    for g in range(plan.groups):
        at = lanes_of(plan, g)
        output_ref[:, at] = (attended_ref[:, at] * norm * gain_ref[:, at]).astype(BF16)
        queries, keys, values = queries_ref[:, at], keys_ref[:, at], values_ref[:, at]
        grads = attended_grad_ref[:, at]
        weighted_ref[:, at] = (values.astype(F32) * exits[:, at]).astype(BF16)
        scores = dot(stack_heads(plan, grads), values, NT)
        score_grads = []
        for k in range(plan.group):
            h = g * plan.group + k
            mask = jnp.exp(columns[:, h : h + 1] - rows[h : h + 1, :] + bias)
            score_grads.append((scores[k * n : (k + 1) * n] * mask).astype(BF16))
        score_grads = jnp.concatenate(score_grads, axis=1)
        probs = probs_ref[:, g * plan.group * n : (g + 1) * plan.group * n]
        query_grad = dot(score_grads, stack_heads(plan, keys))
        query_grad += reach[:, at] * dot(grads, stack_heads(plan, incoming_ref[:, at]), NT)
        query_grad_ref[:, at] = query_grad.astype(BF16)
        key_local_ref[:, at] = own_heads(plan, dot(score_grads, queries, TN), n)
        value_local_ref[:, at] = own_heads(plan, dot(probs, grads, TN), n)


def finish_kernel(
    plan, key_local_ref, value_local_ref, weighted_values_ref, weighted_keys_ref, *refs
):
    pieces = refs[: plan.pieces]
    key_grad_hbm, value_grad_hbm, state_ref, key_grad_ref, value_grad_ref, key_sems, value_sems = refs[
        plan.pieces :
    ]
    load_pieces(plan, place(plan)[1], pieces, state_ref)
    copies = []
    for g in range(plan.groups):
        at = lanes_of(plan, g)
        later = stack_heads(plan, state_ref[:, at].astype(BF16))
        key_grad = key_local_ref[:, at] + dot(weighted_values_ref[:, at], later, NT)
        key_grad_ref[:, at] = key_grad.astype(BF16)
        copies.append(
            pltpu.make_async_copy(key_grad_ref.at[:, at], key_grad_hbm.at[:, at], key_sems.at[g])
        )
        copies[-1].start()
        value_grad = value_local_ref[:, at] + dot(weighted_keys_ref[:, at], later)
        value_grad_ref[:, at] = value_grad.astype(BF16)
        copies.append(
            pltpu.make_async_copy(value_grad_ref.at[:, at], value_grad_hbm.at[:, at], value_sems.at[g])
        )
        copies[-1].start()
    for copy in copies:
        copy.wait()


SCALAR = pl.BlockSpec(memory_space=pltpu.SMEM)
WHOLE = pl.BlockSpec(memory_space=pltpu.VMEM)
FAR = pl.BlockSpec(memory_space=pltpu.HBM)


def call(kernel, name, scalars, arrays, outs, scratch=(), flops=0, far_in=0, far_out=False):
    scalars = [pltpu.with_memory_space_constraint(a, pltpu.HBM) for a in scalars]
    arrays = [
        pltpu.with_memory_space_constraint(a, pltpu.HBM) if i < far_in else a for i, a in enumerate(arrays)
    ]
    moved = sum(a.size * a.dtype.itemsize for a in (*arrays, *outs))
    return pl.pallas_call(
        kernel,
        name=name,
        out_shape=outs,
        in_specs=[SCALAR] * len(scalars) + [FAR] * far_in + [WHOLE] * (len(arrays) - far_in),
        out_specs=[FAR if far_out else WHOLE] * len(outs),
        scratch_shapes=list(scratch),
        compiler_params=pltpu.CompilerParams(vmem_limit_bytes=40 * 2**20),
        cost_estimate=pl.CostEstimate(flops=flops, bytes_accessed=moved, transcendentals=0),
    )(*scalars, *arrays)


def array(*shape, dtype=F32):
    return jax.ShapeDtypeStruct(shape, dtype)


def exchange(pieces, count):
    return [pieces[0]] + [
        lax.ppermute(piece, "ctx", [(i, i ^ m) for i in range(count)])
        for m, piece in enumerate(pieces)
        if m
    ]


def shift(x, count, by):
    pairs = [(i, i + by) for i in range(count) if 0 <= i + by < count]
    return lax.ppermute(x, "ctx", pairs)


def scan_whole(plan, state, factor, count, reach, sign):
    held = shift(state, count, sign)
    rates = shift(factor, count, sign)
    by = 1
    while by < reach:
        held = held + rates * shift(held, count, sign * by)
        rates = rates * shift(rates, count, sign * by)
        by *= 2
    return held


def on_device(queries, keys, values, decay_log, norm_gain, out_grad, doc_lengths):
    tokens, width = queries.shape
    heads = decay_log.shape[0]
    count = lax.axis_size("ctx")
    features = width * lax.axis_size("head")
    reach = count // 4
    even = reach & (reach - 1) == 0 and (width // heads) % (8 * reach) == 0
    plan = Plan(tokens, width, heads, reach if even else 1)
    n = plan.pieces
    gain = norm_gain.reshape(1, width)
    like = array(tokens, width, dtype=BF16)
    wide = array(tokens, width)
    state = pltpu.VMEM((plan.dim, width), F32)
    piece = array(plan.piece_rows, 128)
    framed = array(plan.piece_rows + plan.factor_rows, 128)

    *pieces, weighted_keys = call(
        functools.partial(exit_kernel, plan),
        "exit_states",
        (),
        (doc_lengths, decay_log, keys, values),
        [framed] * n + [like],
        [
            pltpu.SMEM(doc_lengths.shape, jnp.int32),
            pltpu.VMEM(decay_log.shape, F32),
            pltpu.VMEM((tokens, width), BF16),
            pltpu.VMEM((tokens, width), BF16),
            state,
            pltpu.SemaphoreType.DMA((2,)),
            pltpu.SemaphoreType.DMA((1,)),
            pltpu.SemaphoreType.DMA((1,)),
        ],
        flops=10**8,
        far_in=4,
    )
    if even:
        pieces = exchange(pieces, count)
    frames = pieces

    def chain(pieces, reverse, carry=None):
        with_carry = carry is not None
        return call(
            functools.partial(chain_kernel, plan, reverse, with_carry),
            "prefix_states" if with_carry else "total_state",
            (),
            (*pieces, *frames, carry) if with_carry else (*pieces, *frames),
            [piece] * n if with_carry else [piece],
        )

    def entering(pieces, reverse):
        sign = -1 if reverse else 1
        if not even:
            whole = pieces[0][: plan.piece_rows].reshape(plan.tiles, plan.rows, 128)
            factor = frames[0][plan.piece_rows : plan.piece_rows + plan.tiles, None, :]
            return [scan_whole(plan, whole, factor, count, reach, sign).reshape(piece.shape)]
        (total,) = chain(pieces, reverse)
        carry = shift(total, count, sign * n)
        return exchange(chain(pieces, reverse, carry), count)

    incoming = entering(pieces, False)
    probs, local, reached = call(
        functools.partial(local_kernel, plan),
        "local_attention",
        (doc_lengths,),
        (decay_log, queries, keys, values),
        [array(tokens, heads * tokens, dtype=BF16), wide, like],
        flops=10**9,
    )
    attended, sums, incoming_state = call(
        functools.partial(attend_kernel, plan),
        "attended",
        (),
        (local, reached, out_grad, gain, *incoming),
        [wide, array(tokens, 128), array(plan.dim, width, dtype=BF16)],
        [state],
    )
    other = lax.ppermute(sums, "head", [(0, 1), (1, 0)])
    *pieces, attended_grad, norm = call(
        functools.partial(grad_kernel, plan, features),
        "attended_grad",
        (),
        (attended, out_grad, gain, sums, other, reached),
        [piece] * n + [like, array(tokens, 128)],
        [state],
    )
    if even:
        pieces = exchange(pieces, count)
    later = entering(pieces, True)
    output, query_grad, key_local, value_local, weighted_values = call(
        functools.partial(inner_kernel, plan),
        "local_grads",
        (doc_lengths,),
        (
            decay_log,
            queries,
            keys,
            values,
            gain,
            attended,
            attended_grad,
            norm,
            probs,
            incoming_state,
        ),
        [like, like, wide, wide, like],
        flops=10**9,
    )
    key_grad, value_grad = call(
        functools.partial(finish_kernel, plan),
        "key_value_grads",
        (),
        (key_local, value_local, weighted_values, weighted_keys, *later),
        [like, like],
        [
            state,
            pltpu.VMEM((tokens, width), BF16),
            pltpu.VMEM((tokens, width), BF16),
            pltpu.SemaphoreType.DMA((plan.groups,)),
            pltpu.SemaphoreType.DMA((plan.groups,)),
        ],
        far_out=True,
    )
    return (output, query_grad, key_grad, value_grad)


def solution(mesh):
    in_specs = (
        P("ctx", "head"),
        P("ctx", "head"),
        P("ctx", "head"),
        P("head", "ctx"),
        P("head"),
        P("ctx", "head"),
        P(),
    )
    out_specs = (P("ctx", "head"), P("ctx", "head"), P("ctx", "head"), P("ctx", "head"))
    return jax.shard_map(
        on_device, mesh=mesh, in_specs=in_specs, out_specs=out_specs, check_vma=False
    )
```

```python
import functools
import math

import jax
import jax.numpy as jnp
from jax import lax
from jax.experimental import pallas as pl
from jax.experimental.pallas import tpu as pltpu
from jax.sharding import PartitionSpec as P

EPSILON = 1e-06
NEVER = -1e30
F32 = jnp.float32
BF16 = jnp.bfloat16
NN = (((1,), (0,)), ((), ()))
NT = (((1,), (1,)), ((), ()))
TN = (((0,), (0,)), ((), ()))


def dot(a, b, dims=NN):
    return lax.dot_general(a, b, dims, preferred_element_type=F32)


def split3(x):
    a = x.astype(BF16)
    rest = x - a.astype(F32)
    b = rest.astype(BF16)
    return a, b, (rest - b.astype(F32)).astype(BF16)


def exact_dot(x, ones, dims, x_first):
    out = None
    for part in split3(x):
        term = dot(part, ones, dims) if x_first else dot(ones, part, dims)
        out = term if out is None else out + term
    return out


class Plan:
    def __init__(self, tokens, width, heads, pieces):
        self.tokens, self.width, self.heads = tokens, width, heads
        self.dim = width // heads
        self.group = math.lcm(self.dim, 128) // self.dim
        self.lanes = self.group * self.dim
        self.groups = heads // self.group
        self.pieces = pieces
        self.rows = self.dim // pieces
        self.tiles = width // 128
        self.scale = 1.0 / math.sqrt(self.dim)
        self.piece_rows = self.tiles * self.rows
        self.factor_rows = -(-self.tiles // 8) * 8


def place(plan):
    index = lax.axis_index("ctx")
    return index * plan.tokens, lax.rem(index, plan.pieces)


def iota(shape, dim):
    return lax.broadcasted_iota(jnp.int32, shape, dim)


def tri(n, keep):
    return keep(iota((n, n), 0), iota((n, n), 1)).astype(F32).astype(BF16)


def head_mask(plan, k):
    lane = iota((1, plan.lanes), 1)
    return (lane >= k * plan.dim) & (lane < (k + 1) * plan.dim)


def spread(plan, columns):
    head, lane = iota((plan.heads, plan.width), 0), iota((plan.heads, plan.width), 1)
    ones = ((lane >= head * plan.dim) & (lane < (head + 1) * plan.dim)).astype(F32).astype(BF16)
    high = columns.astype(BF16)
    low = (columns - high.astype(F32)).astype(BF16)
    return dot(high, ones) + dot(low, ones)


def doc_edges(plan, lengths_ref, block_start):
    start = jnp.int32(0)
    last, first = jnp.int32(0), jnp.int32(2**30)
    for i in range(lengths_ref.shape[0]):
        last = jnp.where(start < block_start + plan.tokens, start, last)
        first = jnp.where(start >= block_start, jnp.minimum(first, start), first)
        start = start + lengths_ref[i]
    return last, first


def doc_index(lengths_ref, positions):
    start = jnp.int32(0)
    index = jnp.zeros(positions.shape, jnp.int32)
    for i in range(lengths_ref.shape[0]):
        index = index + (positions >= start).astype(jnp.int32)
        start = start + lengths_ref[i]
    return index


def exit_columns(plan, decay, last, block_start):
    after = tri(plan.tokens, lambda t, u: u > t)
    keep = block_start + iota((plan.tokens, plan.heads), 0) >= last
    return jnp.where(keep, jnp.exp(exact_dot(decay, after, NT, False)), 0.0)


def reach_columns(plan, decay, first, block_start):
    until = tri(plan.tokens, lambda t, u: u <= t)
    carry = block_start + iota((plan.tokens, plan.heads), 0) < first
    return jnp.where(carry, jnp.exp(exact_dot(decay, until, NT, False)), 0.0)


def decay_bias(plan, lengths_ref, block_start):
    n = plan.tokens
    t, s = iota((n, n), 0), iota((n, n), 1)
    same = doc_index(lengths_ref, t + block_start) == doc_index(lengths_ref, s + block_start)
    return jnp.where(same & (t >= s), math.log(plan.scale), NEVER)


def log_sums(plan, decay):
    until = tri(plan.tokens, lambda t, u: u <= t)
    return exact_dot(decay, until, NT, False), exact_dot(decay, until, NT, True)


def own_heads(plan, product, rows):
    out = product[:rows]
    for k in range(1, plan.group):
        out = jnp.where(head_mask(plan, k), product[k * rows : (k + 1) * rows], out)
    return out


def stack_heads(plan, x):
    return jnp.concatenate(
        [jnp.where(head_mask(plan, k), x, jnp.zeros_like(x)) for k in range(plan.group)], axis=0
    )


def windows(plan):
    for h in range(0, plan.group, 2):
        heads = range(h, min(h + 2, plan.group))
        start = heads[0] * plan.dim // 128 * 128
        yield heads, start, -(-(heads[-1] + 1) * plan.dim // 128) * 128


def block_diagonal(plan, x, heads, start, stop):
    zeros = lambda rows: [jnp.zeros((rows, stop - start), x.dtype)] if rows else []
    x = x[:, start:stop]
    lane = iota((1, stop - start), 1) + start
    parts = zeros(heads[0] * plan.dim - start)
    for h in heads:
        on = (lane >= h * plan.dim) & (lane < (h + 1) * plan.dim)
        parts.append(jnp.where(on, x, jnp.zeros_like(x)))
    parts += zeros(stop - (heads[-1] + 1) * plan.dim)
    return jnp.concatenate(parts, axis=0)


def sum_windows(plan, terms):
    tiles = [None] * (plan.lanes // 128)
    for start, stop, term in terms:
        for j in range(start // 128, stop // 128):
            tile = term[:, j * 128 - start : (j + 1) * 128 - start]
            tiles[j] = tile if tiles[j] is None else tiles[j] + tile
    return jnp.concatenate(tiles, axis=1)


def through_states(plan, x, state, dims):
    return sum_windows(
        plan,
        [
            (start, stop, dot(x[:, start:stop], block_diagonal(plan, state, heads, start, stop), dims))
            for heads, start, stop in windows(plan)
        ],
    )


def outer_states(plan, x, y):
    terms = []
    for heads, start, stop in windows(plan):
        product = dot(x[:, start:stop], y[:, start:stop], TN)
        lane = iota((1, stop - start), 1) + start
        out = jnp.zeros((plan.dim, stop - start), F32)
        for h in heads:
            on = (lane >= h * plan.dim) & (lane < (h + 1) * plan.dim)
            out = jnp.where(on, product[h * plan.dim - start : (h + 1) * plan.dim - start], out)
        terms.append((start, stop, out))
    return sum_windows(plan, terms)


def lanes_of(plan, g):
    return slice(g * plan.lanes, (g + 1) * plan.lanes)


def store_pieces(plan, mine, state_ref, piece_refs):
    for m, piece in enumerate(piece_refs):
        start = pl.multiple_of((mine ^ m) * plan.rows, plan.rows)
        for j in range(plan.tiles):
            piece[j * plan.rows : (j + 1) * plan.rows, :] = state_ref[
                pl.ds(start, plan.rows), j * 128 : (j + 1) * 128
            ]


def load_pieces(plan, mine, piece_refs, state_ref):
    for m, piece in enumerate(piece_refs):
        start = pl.multiple_of((mine ^ m) * plan.rows, plan.rows)
        for j in range(plan.tiles):
            state_ref[pl.ds(start, plan.rows), j * 128 : (j + 1) * 128] = piece[
                j * plan.rows : (j + 1) * plan.rows, :
            ]


def row_copies(source, target, sems):
    count = sems.shape[0]
    rows = source.shape[0] // count
    return [
        pltpu.make_async_copy(
            source.at[i * rows : (i + 1) * rows], target.at[i * rows : (i + 1) * rows], sems.at[i]
        )
        for i in range(count)
    ]


def exit_kernel(plan, lengths_hbm, decay_hbm, keys_hbm, values_hbm, *refs):
    pieces = refs[: plan.pieces]
    weighted_ref, lengths_ref, decay_ref, keys_ref, values_ref, state_ref, small_sems, key_sems, value_sems = refs[
        plan.pieces :
    ]
    lengths_copy = pltpu.make_async_copy(lengths_hbm, lengths_ref, small_sems.at[0])
    decay_copy = pltpu.make_async_copy(decay_hbm, decay_ref, small_sems.at[1])
    lengths_copy.start()
    decay_copy.start()
    keys_copies = row_copies(keys_hbm, keys_ref, key_sems)
    values_copies = row_copies(values_hbm, values_ref, value_sems)
    for copy in keys_copies + values_copies:
        copy.start()
    block_start, mine = place(plan)
    lengths_copy.wait()
    last, first = doc_edges(plan, lengths_ref, block_start)
    decay_copy.wait()
    decay = decay_ref[...]
    weights = spread(plan, exit_columns(plan, decay, last, block_start))
    whole = jnp.exp(jnp.sum(decay, axis=1, keepdims=True))
    whole = jnp.where(first >= block_start + plan.tokens, whole, 0.0)
    head = iota((plan.heads, 128), 0)
    rows = []
    for j in range(plan.tiles):
        lane = iota((plan.heads, 128), 1) + j * 128
        on = (lane >= head * plan.dim) & (lane < (head + 1) * plan.dim)
        rows.append(jnp.sum(jnp.where(on, whole, 0.0), axis=0, keepdims=True))
    rows.append(jnp.zeros((plan.factor_rows - plan.tiles, 128), F32))
    rows = jnp.concatenate(rows, axis=0)
    for piece in pieces:
        piece[plan.piece_rows :, :] = rows
    for copy in keys_copies:
        copy.wait()
    weighted_ref[...] = (keys_ref[...].astype(F32) * weights).astype(BF16)
    for copy in values_copies:
        copy.wait()
    for g in range(plan.groups):
        at = lanes_of(plan, g)
        state_ref[:, at] = outer_states(plan, weighted_ref[:, at], values_ref[:, at])
    store_pieces(plan, mine, state_ref, pieces)


def chain_kernel(plan, reverse, with_carry, groups, *refs):
    n, rows = plan.pieces, plan.rows
    pieces, factors = refs[:n], refs[n : 2 * n]
    hops = refs[2 * n : 2 * n + 2]
    outs = refs[2 * n + 2 :] if with_carry else refs[2 * n :]
    group = lax.axis_index("ctx") // n
    end = groups - 1 if reverse else 0
    by_first = lax.rem(group, 2) == (0 if reverse else 1)
    order = range(n - 1, -1, -1) if reverse else range(n)

    def at_place(mine):
        for j in range(plan.tiles):
            at = slice(j * rows, (j + 1) * rows)
            tile = None
            if with_carry:
                tile = jnp.where(group == end, 0.0, jnp.where(by_first, hops[0][at], hops[1][at]))
            for step, b in enumerate(order):
                m = mine ^ b
                if with_carry:
                    outs[m][at] = tile
                    if step == n - 1:
                        break
                rate = factors[m][plan.piece_rows + j : plan.piece_rows + j + 1, :]
                tile = pieces[m][at] if tile is None else tile * rate + pieces[m][at]
            if not with_carry:
                outs[0][at] = tile

    own = place(plan)[1]
    for mine in range(n):
        pl.when(own == mine)(functools.partial(at_place, mine))


def local_kernel(
    plan, lengths_ref, decay_ref, queries_ref, keys_ref, values_ref, probs_ref, local_ref, reached_ref
):
    block_start = place(plan)[0]
    decay = decay_ref[...]
    last, first = doc_edges(plan, lengths_ref, block_start)
    columns, rows = log_sums(plan, decay)
    bias = decay_bias(plan, lengths_ref, block_start)
    carry = block_start + iota(columns.shape, 0) < first
    reach = spread(plan, jnp.where(carry, jnp.exp(columns), 0.0) * plan.scale)
    n = plan.tokens
    for g in range(plan.groups):
        at = lanes_of(plan, g)
        queries, keys, values = queries_ref[:, at], keys_ref[:, at], values_ref[:, at]
        reached_ref[:, at] = (queries.astype(F32) * reach[:, at]).astype(BF16)
        scores = dot(stack_heads(plan, queries), keys, NT)
        probs = []
        for k in range(plan.group):
            h = g * plan.group + k
            mask = jnp.exp(columns[:, h : h + 1] - rows[h : h + 1, :] + bias)
            probs.append((scores[k * n : (k + 1) * n] * mask).astype(BF16))
        probs = jnp.concatenate(probs, axis=1)
        probs_ref[:, g * plan.group * n : (g + 1) * plan.group * n] = probs
        local_ref[:, at] = dot(probs, stack_heads(plan, values))


def attend_kernel(plan, local_ref, reached_ref, out_grad_ref, gain_ref, *refs):
    pieces = refs[: plan.pieces]
    attended_ref, sums_ref, incoming_ref, state_ref = refs[plan.pieces :]
    load_pieces(plan, place(plan)[1], pieces, state_ref)
    squares = inner = None
    for g in range(plan.groups):
        at = lanes_of(plan, g)
        incoming = state_ref[:, at].astype(BF16)
        incoming_ref[:, at] = incoming
        attended = local_ref[:, at] + through_states(plan, reached_ref[:, at], incoming, NN)
        attended_ref[:, at] = attended
        grad = out_grad_ref[:, at].astype(F32) * gain_ref[:, at]
        square, product = attended * attended, grad * attended
        for j in range(0, plan.lanes, 128):
            squares = square[:, j : j + 128] if squares is None else squares + square[:, j : j + 128]
            inner = product[:, j : j + 128] if inner is None else inner + product[:, j : j + 128]
    lane = iota((plan.tokens, 128), 1)
    sums_ref[...] = jnp.where(
        lane < 64, jnp.sum(squares, axis=1, keepdims=True), jnp.sum(inner, axis=1, keepdims=True)
    )


def grad_kernel(
    plan, features, attended_ref, out_grad_ref, gain_ref, sums_ref, other_ref, reached_ref, *refs
):
    pieces, (attended_grad_ref, norm_ref, state_ref) = refs[: plan.pieces], refs[plan.pieces :]
    sums = sums_ref[...] + other_ref[...]
    inverse = lax.rsqrt(sums[:, :1] / features + EPSILON)
    norm_ref[...] = jnp.broadcast_to(inverse, norm_ref.shape)
    slope = inverse * inverse * inverse * sums[:, 64:65] / features
    for g in range(plan.groups):
        at = lanes_of(plan, g)
        grad = out_grad_ref[:, at].astype(F32) * gain_ref[:, at]
        attended_grad = (grad * inverse - attended_ref[:, at] * slope).astype(BF16)
        attended_grad_ref[:, at] = attended_grad
        state_ref[:, at] = outer_states(plan, reached_ref[:, at], attended_grad)
    store_pieces(plan, place(plan)[1], state_ref, pieces)


def inner_kernel(
    plan,
    lengths_ref,
    decay_ref,
    queries_ref,
    keys_ref,
    values_ref,
    gain_ref,
    attended_ref,
    attended_grad_ref,
    norm_ref,
    probs_ref,
    incoming_ref,
    output_ref,
    query_grad_ref,
    key_local_ref,
    value_local_ref,
    weighted_ref,
):
    block_start = place(plan)[0]
    decay = decay_ref[...]
    last, first = doc_edges(plan, lengths_ref, block_start)
    columns, rows = log_sums(plan, decay)
    bias = decay_bias(plan, lengths_ref, block_start)
    position = block_start + iota(columns.shape, 0)
    reach = spread(plan, jnp.where(position < first, jnp.exp(columns), 0.0) * plan.scale)
    exits = spread(plan, exit_columns(plan, decay, last, block_start))
    norm = norm_ref[:, :1]
    n = plan.tokens
    for g in range(plan.groups):
        at = lanes_of(plan, g)
        output_ref[:, at] = (attended_ref[:, at] * norm * gain_ref[:, at]).astype(BF16)
        queries, keys, values = queries_ref[:, at], keys_ref[:, at], values_ref[:, at]
        grads = attended_grad_ref[:, at]
        weighted_ref[:, at] = (values.astype(F32) * exits[:, at]).astype(BF16)
        scores = dot(stack_heads(plan, grads), values, NT)
        score_grads = []
        for k in range(plan.group):
            h = g * plan.group + k
            mask = jnp.exp(columns[:, h : h + 1] - rows[h : h + 1, :] + bias)
            score_grads.append((scores[k * n : (k + 1) * n] * mask).astype(BF16))
        score_grads = jnp.concatenate(score_grads, axis=1)
        probs = probs_ref[:, g * plan.group * n : (g + 1) * plan.group * n]
        query_grad = dot(score_grads, stack_heads(plan, keys))
        query_grad += reach[:, at] * through_states(plan, grads, incoming_ref[:, at], NT)
        query_grad_ref[:, at] = query_grad.astype(BF16)
        key_local_ref[:, at] = own_heads(plan, dot(score_grads, queries, TN), n)
        value_local_ref[:, at] = own_heads(plan, dot(probs, grads, TN), n)


def finish_kernel(
    plan, key_local_ref, value_local_ref, weighted_values_ref, weighted_keys_ref, *refs
):
    pieces = refs[: plan.pieces]
    key_grad_hbm, value_grad_hbm, state_ref, key_grad_ref, value_grad_ref, key_sems, value_sems = refs[
        plan.pieces :
    ]
    load_pieces(plan, place(plan)[1], pieces, state_ref)
    copies = []
    for g in range(plan.groups):
        at = lanes_of(plan, g)
        later = state_ref[:, at].astype(BF16)
        key_grad = key_local_ref[:, at] + through_states(plan, weighted_values_ref[:, at], later, NT)
        key_grad_ref[:, at] = key_grad.astype(BF16)
        copies.append(
            pltpu.make_async_copy(key_grad_ref.at[:, at], key_grad_hbm.at[:, at], key_sems.at[g])
        )
        copies[-1].start()
        value_grad = value_local_ref[:, at] + through_states(plan, weighted_keys_ref[:, at], later, NN)
        value_grad_ref[:, at] = value_grad.astype(BF16)
        copies.append(
            pltpu.make_async_copy(value_grad_ref.at[:, at], value_grad_hbm.at[:, at], value_sems.at[g])
        )
        copies[-1].start()
    for copy in copies:
        copy.wait()


SCALAR = pl.BlockSpec(memory_space=pltpu.SMEM)
WHOLE = pl.BlockSpec(memory_space=pltpu.VMEM)
FAR = pl.BlockSpec(memory_space=pltpu.HBM)


def call(kernel, name, scalars, arrays, outs, scratch=(), flops=0, far_in=0, far_out=False):
    scalars = [pltpu.with_memory_space_constraint(a, pltpu.HBM) for a in scalars]
    arrays = [
        pltpu.with_memory_space_constraint(a, pltpu.HBM) if i < far_in else a for i, a in enumerate(arrays)
    ]
    moved = sum(a.size * a.dtype.itemsize for a in (*arrays, *outs))
    return pl.pallas_call(
        kernel,
        name=name,
        out_shape=outs,
        in_specs=[SCALAR] * len(scalars) + [FAR] * far_in + [WHOLE] * (len(arrays) - far_in),
        out_specs=[FAR if far_out else WHOLE] * len(outs),
        scratch_shapes=list(scratch),
        compiler_params=pltpu.CompilerParams(vmem_limit_bytes=40 * 2**20),
        cost_estimate=pl.CostEstimate(flops=flops, bytes_accessed=moved, transcendentals=0),
    )(*scalars, *arrays)


def array(*shape, dtype=F32):
    return jax.ShapeDtypeStruct(shape, dtype)


def exchange(pieces, count):
    return [pieces[0]] + [
        lax.ppermute(piece, "ctx", [(i, i ^ m) for i in range(count)])
        for m, piece in enumerate(pieces)
        if m
    ]


def shift(x, count, by):
    pairs = [(i, i + by) for i in range(count) if 0 <= i + by < count]
    return lax.ppermute(x, "ctx", pairs)


def group_swaps(n, count):
    first = [(i, i ^ n) for i in range(count)]
    second = [(i, i ^ 1 if i < n or i >= count - n else (((i // n - 1) ^ 1) + 1) * n + i % n) for i in range(count)]
    return first, second


def scan_whole(plan, state, factor, count, reach, sign):
    held = shift(state, count, sign)
    rates = shift(factor, count, sign)
    by = 1
    while by < reach:
        held = held + rates * shift(held, count, sign * by)
        rates = rates * shift(rates, count, sign * by)
        by *= 2
    return held


def on_device(queries, keys, values, decay_log, norm_gain, out_grad, doc_lengths):
    tokens, width = queries.shape
    heads = decay_log.shape[0]
    count = lax.axis_size("ctx")
    features = width * lax.axis_size("head")
    reach = count // 4
    even = reach > 1 and reach & (reach - 1) == 0 and (width // heads) % (8 * reach) == 0
    plan = Plan(tokens, width, heads, reach if even else 1)
    n = plan.pieces
    gain = norm_gain.reshape(1, width)
    like = array(tokens, width, dtype=BF16)
    wide = array(tokens, width)
    state = pltpu.VMEM((plan.dim, width), F32)
    piece = array(plan.piece_rows, 128)
    framed = array(plan.piece_rows + plan.factor_rows, 128)

    *pieces, weighted_keys = call(
        functools.partial(exit_kernel, plan),
        "exit_states",
        (),
        (doc_lengths, decay_log, keys, values),
        [framed] * n + [like],
        [
            pltpu.SMEM(doc_lengths.shape, jnp.int32),
            pltpu.VMEM(decay_log.shape, F32),
            pltpu.VMEM((tokens, width), BF16),
            pltpu.VMEM((tokens, width), BF16),
            state,
            pltpu.SemaphoreType.DMA((2,)),
            pltpu.SemaphoreType.DMA((1,)),
            pltpu.SemaphoreType.DMA((1,)),
        ],
        flops=10**8,
        far_in=4,
    )
    if even:
        pieces = exchange(pieces, count)
    frames = pieces

    def chain(pieces, reverse, carry=None):
        with_carry = carry is not None
        return call(
            functools.partial(chain_kernel, plan, reverse, with_carry, count // n),
            "prefix_states" if with_carry else "total_state",
            (),
            (*pieces, *frames, *carry) if with_carry else (*pieces, *frames),
            [piece] * n if with_carry else [piece],
        )

    def entering(pieces, reverse):
        sign = -1 if reverse else 1
        if not even:
            whole = pieces[0][: plan.piece_rows].reshape(plan.tiles, plan.rows, 128)
            factor = frames[0][plan.piece_rows : plan.piece_rows + plan.tiles, None, :]
            return [scan_whole(plan, whole, factor, count, reach, sign).reshape(piece.shape)]
        (total,) = chain(pieces, reverse)
        carry = [lax.ppermute(total, "ctx", pairs) for pairs in group_swaps(n, count)]
        return exchange(chain(pieces, reverse, carry), count)

    incoming = entering(pieces, False)
    probs, local, reached = call(
        functools.partial(local_kernel, plan),
        "local_attention",
        (doc_lengths,),
        (decay_log, queries, keys, values),
        [array(tokens, heads * tokens, dtype=BF16), wide, like],
        flops=10**9,
    )
    attended, sums, incoming_state = call(
        functools.partial(attend_kernel, plan),
        "attended",
        (),
        (local, reached, out_grad, gain, *incoming),
        [wide, array(tokens, 128), array(plan.dim, width, dtype=BF16)],
        [state],
    )
    other = lax.ppermute(sums, "head", [(0, 1), (1, 0)])
    *pieces, attended_grad, norm = call(
        functools.partial(grad_kernel, plan, features),
        "attended_grad",
        (),
        (attended, out_grad, gain, sums, other, reached),
        [piece] * n + [like, array(tokens, 128)],
        [state],
    )
    if even:
        pieces = exchange(pieces, count)
    later = entering(pieces, True)
    output, query_grad, key_local, value_local, weighted_values = call(
        functools.partial(inner_kernel, plan),
        "local_grads",
        (doc_lengths,),
        (
            decay_log,
            queries,
            keys,
            values,
            gain,
            attended,
            attended_grad,
            norm,
            probs,
            incoming_state,
        ),
        [like, like, wide, wide, like],
        flops=10**9,
    )
    key_grad, value_grad = call(
        functools.partial(finish_kernel, plan),
        "key_value_grads",
        (),
        (key_local, value_local, weighted_values, weighted_keys, *later),
        [like, like],
        [
            state,
            pltpu.VMEM((tokens, width), BF16),
            pltpu.VMEM((tokens, width), BF16),
            pltpu.SemaphoreType.DMA((plan.groups,)),
            pltpu.SemaphoreType.DMA((plan.groups,)),
        ],
        far_out=True,
    )
    return (output, query_grad, key_grad, value_grad)


def solution(mesh):
    in_specs = (
        P("ctx", "head"),
        P("ctx", "head"),
        P("ctx", "head"),
        P("head", "ctx"),
        P("head"),
        P("ctx", "head"),
        P(),
    )
    out_specs = (P("ctx", "head"), P("ctx", "head"), P("ctx", "head"), P("ctx", "head"))
    return jax.shard_map(
        on_device, mesh=mesh, in_specs=in_specs, out_specs=out_specs, check_vma=False
    )
```

```python
import functools
import math

import jax
import jax.numpy as jnp
from jax import lax
from jax.experimental import pallas as pl
from jax.experimental.pallas import tpu as pltpu
from jax.sharding import PartitionSpec as P

EPSILON = 1e-06
NEVER = -1e30
F32 = jnp.float32
BF16 = jnp.bfloat16
NN = (((1,), (0,)), ((), ()))
NT = (((1,), (1,)), ((), ()))
TN = (((0,), (0,)), ((), ()))


def dot(a, b, dims=NN):
    return lax.dot_general(a, b, dims, preferred_element_type=F32)


def split3(x):
    a = x.astype(BF16)
    rest = x - a.astype(F32)
    b = rest.astype(BF16)
    return a, b, (rest - b.astype(F32)).astype(BF16)


def exact_dot(x, ones, dims, x_first):
    out = None
    for part in split3(x):
        term = dot(part, ones, dims) if x_first else dot(ones, part, dims)
        out = term if out is None else out + term
    return out


class Plan:
    def __init__(self, tokens, width, heads, pieces):
        self.tokens, self.width, self.heads = tokens, width, heads
        self.dim = width // heads
        self.group = math.lcm(self.dim, 128) // self.dim
        self.lanes = self.group * self.dim
        self.groups = heads // self.group
        self.pieces = pieces
        self.out_masks = tuple(range(pieces))
        self.back_masks = (0, *range(pieces - 1, 0, -1)) if pieces != 4 else (0, 3, 1, 2)
        self.rows = self.dim // pieces
        self.tiles = width // 128
        self.scale = 1.0 / math.sqrt(self.dim)
        self.piece_rows = self.tiles * self.rows
        self.factor_rows = -(-self.tiles // 8) * 8


def place(plan):
    index = lax.axis_index("ctx")
    return index * plan.tokens, lax.rem(index, plan.pieces)


def iota(shape, dim):
    return lax.broadcasted_iota(jnp.int32, shape, dim)


def tri(n, keep):
    return keep(iota((n, n), 0), iota((n, n), 1)).astype(F32).astype(BF16)


def head_mask(plan, k):
    lane = iota((1, plan.lanes), 1)
    return (lane >= k * plan.dim) & (lane < (k + 1) * plan.dim)


def spread(plan, columns):
    head, lane = iota((plan.heads, plan.width), 0), iota((plan.heads, plan.width), 1)
    ones = ((lane >= head * plan.dim) & (lane < (head + 1) * plan.dim)).astype(F32).astype(BF16)
    high = columns.astype(BF16)
    low = (columns - high.astype(F32)).astype(BF16)
    return dot(high, ones) + dot(low, ones)


def doc_edges(plan, lengths_ref, block_start):
    start = jnp.int32(0)
    last, first = jnp.int32(0), jnp.int32(2**30)
    for i in range(lengths_ref.shape[0]):
        last = jnp.where(start < block_start + plan.tokens, start, last)
        first = jnp.where(start >= block_start, jnp.minimum(first, start), first)
        start = start + lengths_ref[i]
    return last, first


def doc_index(lengths_ref, positions):
    start = jnp.int32(0)
    index = jnp.zeros(positions.shape, jnp.int32)
    for i in range(lengths_ref.shape[0]):
        index = index + (positions >= start).astype(jnp.int32)
        start = start + lengths_ref[i]
    return index


def exit_columns(plan, decay, last, block_start):
    after = tri(plan.tokens, lambda t, u: u > t)
    keep = block_start + iota((plan.tokens, plan.heads), 0) >= last
    return jnp.where(keep, jnp.exp(exact_dot(decay, after, NT, False)), 0.0)


def reach_columns(plan, decay, first, block_start):
    until = tri(plan.tokens, lambda t, u: u <= t)
    carry = block_start + iota((plan.tokens, plan.heads), 0) < first
    return jnp.where(carry, jnp.exp(exact_dot(decay, until, NT, False)), 0.0)


def decay_bias(plan, lengths_ref, block_start):
    n = plan.tokens
    t, s = iota((n, n), 0), iota((n, n), 1)
    same = doc_index(lengths_ref, t + block_start) == doc_index(lengths_ref, s + block_start)
    return jnp.where(same & (t >= s), math.log(plan.scale), NEVER)


def log_sums(plan, decay):
    until = tri(plan.tokens, lambda t, u: u <= t)
    return exact_dot(decay, until, NT, False), exact_dot(decay, until, NT, True)


def own_heads(plan, product, rows):
    out = product[:rows]
    for k in range(1, plan.group):
        out = jnp.where(head_mask(plan, k), product[k * rows : (k + 1) * rows], out)
    return out


def stack_heads(plan, x):
    return jnp.concatenate(
        [jnp.where(head_mask(plan, k), x, jnp.zeros_like(x)) for k in range(plan.group)], axis=0
    )


def windows(plan):
    for h in range(0, plan.group, 2):
        heads = range(h, min(h + 2, plan.group))
        start = heads[0] * plan.dim // 128 * 128
        yield heads, start, -(-(heads[-1] + 1) * plan.dim // 128) * 128


def block_diagonal(plan, x, heads, start, stop):
    zeros = lambda rows: [jnp.zeros((rows, stop - start), x.dtype)] if rows else []
    x = x[:, start:stop]
    lane = iota((1, stop - start), 1) + start
    parts = zeros(heads[0] * plan.dim - start)
    for h in heads:
        on = (lane >= h * plan.dim) & (lane < (h + 1) * plan.dim)
        parts.append(jnp.where(on, x, jnp.zeros_like(x)))
    parts += zeros(stop - (heads[-1] + 1) * plan.dim)
    return jnp.concatenate(parts, axis=0)


def sum_windows(plan, terms):
    tiles = [None] * (plan.lanes // 128)
    for start, stop, term in terms:
        for j in range(start // 128, stop // 128):
            tile = term[:, j * 128 - start : (j + 1) * 128 - start]
            tiles[j] = tile if tiles[j] is None else tiles[j] + tile
    return jnp.concatenate(tiles, axis=1)


def through_states(plan, x, state, dims):
    return sum_windows(
        plan,
        [
            (start, stop, dot(x[:, start:stop], block_diagonal(plan, state, heads, start, stop), dims))
            for heads, start, stop in windows(plan)
        ],
    )


def outer_states(plan, x, y):
    terms = []
    for heads, start, stop in windows(plan):
        product = dot(x[:, start:stop], y[:, start:stop], TN)
        lane = iota((1, stop - start), 1) + start
        out = jnp.zeros((plan.dim, stop - start), F32)
        for h in heads:
            on = (lane >= h * plan.dim) & (lane < (h + 1) * plan.dim)
            out = jnp.where(on, product[h * plan.dim - start : (h + 1) * plan.dim - start], out)
        terms.append((start, stop, out))
    return sum_windows(plan, terms)


def lanes_of(plan, g):
    return slice(g * plan.lanes, (g + 1) * plan.lanes)


def store_pieces(plan, mine, state_ref, piece_refs):
    for m, piece in zip(plan.out_masks, piece_refs):
        start = pl.multiple_of((mine ^ m) * plan.rows, plan.rows)
        for j in range(plan.tiles):
            piece[j * plan.rows : (j + 1) * plan.rows, :] = state_ref[
                pl.ds(start, plan.rows), j * 128 : (j + 1) * 128
            ]


def load_pieces(plan, mine, piece_refs, state_ref):
    for m, piece in zip(plan.back_masks, piece_refs):
        start = pl.multiple_of((mine ^ m) * plan.rows, plan.rows)
        for j in range(plan.tiles):
            state_ref[pl.ds(start, plan.rows), j * 128 : (j + 1) * 128] = piece[
                j * plan.rows : (j + 1) * plan.rows, :
            ]


def row_copies(source, target, sems):
    count = sems.shape[0]
    rows = source.shape[0] // count
    return [
        pltpu.make_async_copy(
            source.at[i * rows : (i + 1) * rows], target.at[i * rows : (i + 1) * rows], sems.at[i]
        )
        for i in range(count)
    ]


def exit_kernel(plan, lengths_hbm, decay_hbm, keys_hbm, values_hbm, *refs):
    pieces = refs[: plan.pieces]
    weighted_ref, lengths_ref, decay_ref, keys_ref, values_ref, state_ref, small_sems, key_sems, value_sems = refs[
        plan.pieces :
    ]
    lengths_copy = pltpu.make_async_copy(lengths_hbm, lengths_ref, small_sems.at[0])
    decay_copy = pltpu.make_async_copy(decay_hbm, decay_ref, small_sems.at[1])
    lengths_copy.start()
    decay_copy.start()
    keys_copies = row_copies(keys_hbm, keys_ref, key_sems)
    values_copies = row_copies(values_hbm, values_ref, value_sems)
    for copy in keys_copies + values_copies:
        copy.start()
    block_start, mine = place(plan)
    lengths_copy.wait()
    last, first = doc_edges(plan, lengths_ref, block_start)
    decay_copy.wait()
    decay = decay_ref[...]
    weights = spread(plan, exit_columns(plan, decay, last, block_start))
    whole = jnp.exp(jnp.sum(decay, axis=1, keepdims=True))
    whole = jnp.where(first >= block_start + plan.tokens, whole, 0.0)
    head = iota((plan.heads, 128), 0)
    rows = []
    for j in range(plan.tiles):
        lane = iota((plan.heads, 128), 1) + j * 128
        on = (lane >= head * plan.dim) & (lane < (head + 1) * plan.dim)
        rows.append(jnp.sum(jnp.where(on, whole, 0.0), axis=0, keepdims=True))
    rows.append(jnp.zeros((plan.factor_rows - plan.tiles, 128), F32))
    rows = jnp.concatenate(rows, axis=0)
    for piece in pieces:
        piece[plan.piece_rows :, :] = rows
    for copy in keys_copies:
        copy.wait()
    weighted_ref[...] = (keys_ref[...].astype(F32) * weights).astype(BF16)
    for copy in values_copies:
        copy.wait()
    for g in range(plan.groups):
        at = lanes_of(plan, g)
        state_ref[:, at] = outer_states(plan, weighted_ref[:, at], values_ref[:, at])
    store_pieces(plan, mine, state_ref, pieces)


def chain_kernel(plan, reverse, with_carry, groups, *refs):
    n, rows = plan.pieces, plan.rows
    pieces, factors = refs[:n], refs[n : 2 * n]
    hops = refs[2 * n : 2 * n + 2]
    outs = refs[2 * n + 2 :] if with_carry else refs[2 * n :]
    group = lax.axis_index("ctx") // n
    end = groups - 1 if reverse else 0
    by_first = lax.rem(group, 2) == (0 if reverse else 1)
    order = range(n - 1, -1, -1) if reverse else range(n)

    def at_place(mine):
        for j in range(plan.tiles):
            at = slice(j * rows, (j + 1) * rows)
            tile = None
            if with_carry:
                tile = jnp.where(group == end, 0.0, jnp.where(by_first, hops[0][at], hops[1][at]))
            for step, b in enumerate(order):
                m = plan.out_masks.index(mine ^ b)
                if with_carry:
                    outs[plan.back_masks.index(mine ^ b)][at] = tile
                    if step == n - 1:
                        break
                rate = factors[m][plan.piece_rows + j : plan.piece_rows + j + 1, :]
                tile = pieces[m][at] if tile is None else tile * rate + pieces[m][at]
            if not with_carry:
                outs[0][at] = tile

    own = place(plan)[1]
    for mine in range(n):
        pl.when(own == mine)(functools.partial(at_place, mine))


def local_kernel(
    plan, lengths_ref, decay_ref, queries_ref, keys_ref, values_ref, probs_ref, local_ref, reached_ref
):
    block_start = place(plan)[0]
    decay = decay_ref[...]
    last, first = doc_edges(plan, lengths_ref, block_start)
    columns, rows = log_sums(plan, decay)
    bias = decay_bias(plan, lengths_ref, block_start)
    carry = block_start + iota(columns.shape, 0) < first
    reach = spread(plan, jnp.where(carry, jnp.exp(columns), 0.0) * plan.scale)
    n = plan.tokens
    for g in range(plan.groups):
        at = lanes_of(plan, g)
        queries, keys, values = queries_ref[:, at], keys_ref[:, at], values_ref[:, at]
        reached_ref[:, at] = (queries.astype(F32) * reach[:, at]).astype(BF16)
        scores = dot(stack_heads(plan, queries), keys, NT)
        probs = []
        for k in range(plan.group):
            h = g * plan.group + k
            mask = jnp.exp(columns[:, h : h + 1] - rows[h : h + 1, :] + bias)
            probs.append((scores[k * n : (k + 1) * n] * mask).astype(BF16))
        probs = jnp.concatenate(probs, axis=1)
        probs_ref[:, g * plan.group * n : (g + 1) * plan.group * n] = probs
        local_ref[:, at] = dot(probs, stack_heads(plan, values))


def attend_kernel(plan, local_ref, reached_ref, out_grad_ref, gain_ref, *refs):
    pieces = refs[: plan.pieces]
    attended_ref, sums_ref, incoming_ref, state_ref = refs[plan.pieces :]
    load_pieces(plan, place(plan)[1], pieces, state_ref)
    squares = inner = None
    for g in range(plan.groups):
        at = lanes_of(plan, g)
        incoming = state_ref[:, at].astype(BF16)
        incoming_ref[:, at] = incoming
        attended = local_ref[:, at] + through_states(plan, reached_ref[:, at], incoming, NN)
        attended_ref[:, at] = attended
        grad = out_grad_ref[:, at].astype(F32) * gain_ref[:, at]
        square, product = attended * attended, grad * attended
        for j in range(0, plan.lanes, 128):
            squares = square[:, j : j + 128] if squares is None else squares + square[:, j : j + 128]
            inner = product[:, j : j + 128] if inner is None else inner + product[:, j : j + 128]
    lane = iota((plan.tokens, 128), 1)
    sums_ref[...] = jnp.where(
        lane < 64, jnp.sum(squares, axis=1, keepdims=True), jnp.sum(inner, axis=1, keepdims=True)
    )


def grad_kernel(
    plan, features, attended_ref, out_grad_ref, gain_ref, sums_ref, other_ref, reached_ref, *refs
):
    pieces, (attended_grad_ref, norm_ref, state_ref) = refs[: plan.pieces], refs[plan.pieces :]
    sums = sums_ref[...] + other_ref[...]
    inverse = lax.rsqrt(sums[:, :1] / features + EPSILON)
    norm_ref[...] = jnp.broadcast_to(inverse, norm_ref.shape)
    slope = inverse * inverse * inverse * sums[:, 64:65] / features
    for g in range(plan.groups):
        at = lanes_of(plan, g)
        grad = out_grad_ref[:, at].astype(F32) * gain_ref[:, at]
        attended_grad = (grad * inverse - attended_ref[:, at] * slope).astype(BF16)
        attended_grad_ref[:, at] = attended_grad
        state_ref[:, at] = outer_states(plan, reached_ref[:, at], attended_grad)
    store_pieces(plan, place(plan)[1], state_ref, pieces)


def inner_kernel(
    plan,
    lengths_ref,
    decay_ref,
    queries_ref,
    keys_ref,
    values_ref,
    gain_ref,
    attended_ref,
    attended_grad_ref,
    norm_ref,
    probs_ref,
    incoming_ref,
    output_ref,
    query_grad_ref,
    key_local_ref,
    value_local_ref,
    weighted_ref,
):
    block_start = place(plan)[0]
    decay = decay_ref[...]
    last, first = doc_edges(plan, lengths_ref, block_start)
    columns, rows = log_sums(plan, decay)
    bias = decay_bias(plan, lengths_ref, block_start)
    position = block_start + iota(columns.shape, 0)
    reach = spread(plan, jnp.where(position < first, jnp.exp(columns), 0.0) * plan.scale)
    exits = spread(plan, exit_columns(plan, decay, last, block_start))
    norm = norm_ref[:, :1]
    n = plan.tokens
    for g in range(plan.groups):
        at = lanes_of(plan, g)
        output_ref[:, at] = (attended_ref[:, at] * norm * gain_ref[:, at]).astype(BF16)
        queries, keys, values = queries_ref[:, at], keys_ref[:, at], values_ref[:, at]
        grads = attended_grad_ref[:, at]
        weighted_ref[:, at] = (values.astype(F32) * exits[:, at]).astype(BF16)
        scores = dot(stack_heads(plan, grads), values, NT)
        score_grads = []
        for k in range(plan.group):
            h = g * plan.group + k
            mask = jnp.exp(columns[:, h : h + 1] - rows[h : h + 1, :] + bias)
            score_grads.append((scores[k * n : (k + 1) * n] * mask).astype(BF16))
        score_grads = jnp.concatenate(score_grads, axis=1)
        probs = probs_ref[:, g * plan.group * n : (g + 1) * plan.group * n]
        query_grad = dot(score_grads, stack_heads(plan, keys))
        query_grad += reach[:, at] * through_states(plan, grads, incoming_ref[:, at], NT)
        query_grad_ref[:, at] = query_grad.astype(BF16)
        key_local_ref[:, at] = own_heads(plan, dot(score_grads, queries, TN), n)
        value_local_ref[:, at] = own_heads(plan, dot(probs, grads, TN), n)


def finish_kernel(
    plan, key_local_ref, value_local_ref, weighted_values_ref, weighted_keys_ref, *refs
):
    pieces = refs[: plan.pieces]
    key_grad_hbm, value_grad_hbm, state_ref, key_grad_ref, value_grad_ref, key_sems, value_sems = refs[
        plan.pieces :
    ]
    load_pieces(plan, place(plan)[1], pieces, state_ref)
    copies = []
    for g in range(plan.groups):
        at = lanes_of(plan, g)
        later = state_ref[:, at].astype(BF16)
        key_grad = key_local_ref[:, at] + through_states(plan, weighted_values_ref[:, at], later, NT)
        key_grad_ref[:, at] = key_grad.astype(BF16)
        copies.append(
            pltpu.make_async_copy(key_grad_ref.at[:, at], key_grad_hbm.at[:, at], key_sems.at[g])
        )
        copies[-1].start()
        value_grad = value_local_ref[:, at] + through_states(plan, weighted_keys_ref[:, at], later, NN)
        value_grad_ref[:, at] = value_grad.astype(BF16)
        copies.append(
            pltpu.make_async_copy(value_grad_ref.at[:, at], value_grad_hbm.at[:, at], value_sems.at[g])
        )
        copies[-1].start()
    for copy in copies:
        copy.wait()


SCALAR = pl.BlockSpec(memory_space=pltpu.SMEM)
WHOLE = pl.BlockSpec(memory_space=pltpu.VMEM)
FAR = pl.BlockSpec(memory_space=pltpu.HBM)


def call(kernel, name, scalars, arrays, outs, scratch=(), flops=0, far_in=0, far_out=False):
    scalars = [pltpu.with_memory_space_constraint(a, pltpu.HBM) for a in scalars]
    arrays = [
        pltpu.with_memory_space_constraint(a, pltpu.HBM) if i < far_in else a for i, a in enumerate(arrays)
    ]
    moved = sum(a.size * a.dtype.itemsize for a in (*arrays, *outs))
    return pl.pallas_call(
        kernel,
        name=name,
        out_shape=outs,
        in_specs=[SCALAR] * len(scalars) + [FAR] * far_in + [WHOLE] * (len(arrays) - far_in),
        out_specs=[FAR if far_out else WHOLE] * len(outs),
        scratch_shapes=list(scratch),
        compiler_params=pltpu.CompilerParams(vmem_limit_bytes=40 * 2**20),
        cost_estimate=pl.CostEstimate(flops=flops, bytes_accessed=moved, transcendentals=0),
    )(*scalars, *arrays)


def array(*shape, dtype=F32):
    return jax.ShapeDtypeStruct(shape, dtype)


def exchange(pieces, count, masks):
    return [
        lax.ppermute(piece, "ctx", [(i, i ^ m) for i in range(count)]) if m else piece
        for m, piece in zip(masks, pieces)
    ]


def shift(x, count, by):
    pairs = [(i, i + by) for i in range(count) if 0 <= i + by < count]
    return lax.ppermute(x, "ctx", pairs)


def group_swaps(n, count):
    first = [(i, i ^ n) for i in range(count)]
    second = [(i, i ^ 1 if i < n or i >= count - n else (((i // n - 1) ^ 1) + 1) * n + i % n) for i in range(count)]
    return first, second


def scan_whole(plan, state, factor, count, reach, sign):
    held = shift(state, count, sign)
    rates = shift(factor, count, sign)
    by = 1
    while by < reach:
        held = held + rates * shift(held, count, sign * by)
        rates = rates * shift(rates, count, sign * by)
        by *= 2
    return held


def on_device(queries, keys, values, decay_log, norm_gain, out_grad, doc_lengths):
    tokens, width = queries.shape
    heads = decay_log.shape[0]
    count = lax.axis_size("ctx")
    features = width * lax.axis_size("head")
    reach = count // 4
    even = reach > 1 and reach & (reach - 1) == 0 and (width // heads) % (8 * reach) == 0
    plan = Plan(tokens, width, heads, reach if even else 1)
    n = plan.pieces
    gain = norm_gain.reshape(1, width)
    like = array(tokens, width, dtype=BF16)
    wide = array(tokens, width)
    state = pltpu.VMEM((plan.dim, width), F32)
    piece = array(plan.piece_rows, 128)
    framed = array(plan.piece_rows + plan.factor_rows, 128)

    *pieces, weighted_keys = call(
        functools.partial(exit_kernel, plan),
        "exit_states",
        (),
        (doc_lengths, decay_log, keys, values),
        [framed] * n + [like],
        [
            pltpu.SMEM(doc_lengths.shape, jnp.int32),
            pltpu.VMEM(decay_log.shape, F32),
            pltpu.VMEM((tokens, width), BF16),
            pltpu.VMEM((tokens, width), BF16),
            state,
            pltpu.SemaphoreType.DMA((2,)),
            pltpu.SemaphoreType.DMA((1,)),
            pltpu.SemaphoreType.DMA((1,)),
        ],
        flops=10**8,
        far_in=4,
    )
    if even:
        pieces = exchange(pieces, count, plan.out_masks)
    frames = pieces

    def chain(pieces, reverse, carry=None):
        with_carry = carry is not None
        return call(
            functools.partial(chain_kernel, plan, reverse, with_carry, count // n),
            "prefix_states" if with_carry else "total_state",
            (),
            (*pieces, *frames, *carry) if with_carry else (*pieces, *frames),
            [piece] * n if with_carry else [piece],
        )

    def entering(pieces, reverse):
        sign = -1 if reverse else 1
        if not even:
            whole = pieces[0][: plan.piece_rows].reshape(plan.tiles, plan.rows, 128)
            factor = frames[0][plan.piece_rows : plan.piece_rows + plan.tiles, None, :]
            return [scan_whole(plan, whole, factor, count, reach, sign).reshape(piece.shape)]
        (total,) = chain(pieces, reverse)
        carry = [lax.ppermute(total, "ctx", pairs) for pairs in group_swaps(n, count)]
        return exchange(chain(pieces, reverse, carry), count, plan.back_masks)

    incoming = entering(pieces, False)
    probs, local, reached = call(
        functools.partial(local_kernel, plan),
        "local_attention",
        (doc_lengths,),
        (decay_log, queries, keys, values),
        [array(tokens, heads * tokens, dtype=BF16), wide, like],
        flops=10**9,
    )
    attended, sums, incoming_state = call(
        functools.partial(attend_kernel, plan),
        "attended",
        (),
        (local, reached, out_grad, gain, *incoming),
        [wide, array(tokens, 128), array(plan.dim, width, dtype=BF16)],
        [state],
    )
    other = lax.ppermute(sums, "head", [(0, 1), (1, 0)])
    *pieces, attended_grad, norm = call(
        functools.partial(grad_kernel, plan, features),
        "attended_grad",
        (),
        (attended, out_grad, gain, sums, other, reached),
        [piece] * n + [like, array(tokens, 128)],
        [state],
    )
    if even:
        pieces = exchange(pieces, count, plan.out_masks)
    later = entering(pieces, True)
    output, query_grad, key_local, value_local, weighted_values = call(
        functools.partial(inner_kernel, plan),
        "local_grads",
        (doc_lengths,),
        (
            decay_log,
            queries,
            keys,
            values,
            gain,
            attended,
            attended_grad,
            norm,
            probs,
            incoming_state,
        ),
        [like, like, wide, wide, like],
        flops=10**9,
    )
    key_grad, value_grad = call(
        functools.partial(finish_kernel, plan),
        "key_value_grads",
        (),
        (key_local, value_local, weighted_values, weighted_keys, *later),
        [like, like],
        [
            state,
            pltpu.VMEM((tokens, width), BF16),
            pltpu.VMEM((tokens, width), BF16),
            pltpu.SemaphoreType.DMA((plan.groups,)),
            pltpu.SemaphoreType.DMA((plan.groups,)),
        ],
        far_out=True,
    )
    return (output, query_grad, key_grad, value_grad)


def solution(mesh):
    in_specs = (
        P("ctx", "head"),
        P("ctx", "head"),
        P("ctx", "head"),
        P("head", "ctx"),
        P("head"),
        P("ctx", "head"),
        P(),
    )
    out_specs = (P("ctx", "head"), P("ctx", "head"), P("ctx", "head"), P("ctx", "head"))
    return jax.shard_map(
        on_device, mesh=mesh, in_specs=in_specs, out_specs=out_specs, check_vma=False
    )
```

```python
import functools
import math

import jax
import jax.numpy as jnp
from jax import lax
from jax.experimental import pallas as pl
from jax.experimental.pallas import tpu as pltpu
from jax.sharding import PartitionSpec as P

EPSILON = 1e-06
NEVER = -1e30
F32 = jnp.float32
BF16 = jnp.bfloat16
NN = (((1,), (0,)), ((), ()))
NT = (((1,), (1,)), ((), ()))
TN = (((0,), (0,)), ((), ()))


def dot(a, b, dims=NN):
    return lax.dot_general(a, b, dims, preferred_element_type=F32)


def split3(x):
    a = x.astype(BF16)
    rest = x - a.astype(F32)
    b = rest.astype(BF16)
    return a, b, (rest - b.astype(F32)).astype(BF16)


def exact_dot(x, ones, dims, x_first):
    out = None
    for part in split3(x):
        term = dot(part, ones, dims) if x_first else dot(ones, part, dims)
        out = term if out is None else out + term
    return out


class Plan:
    def __init__(self, tokens, width, heads, pieces):
        self.tokens, self.width, self.heads = tokens, width, heads
        self.dim = width // heads
        self.group = math.lcm(self.dim, 128) // self.dim
        self.lanes = self.group * self.dim
        self.groups = heads // self.group
        self.pieces = pieces
        self.out_masks = tuple(range(pieces))
        self.back_masks = (0, *range(pieces - 1, 0, -1)) if pieces != 4 else (0, 3, 1, 2)
        self.rows = self.dim // pieces
        self.tiles = width // 128
        self.scale = 1.0 / math.sqrt(self.dim)
        self.piece_rows = self.tiles * self.rows
        self.factor_rows = -(-self.tiles // 8) * 8


def place(plan):
    index = lax.axis_index("ctx")
    return index * plan.tokens, lax.rem(index, plan.pieces)


def iota(shape, dim):
    return lax.broadcasted_iota(jnp.int32, shape, dim)


def tri(n, keep):
    return keep(iota((n, n), 0), iota((n, n), 1)).astype(F32).astype(BF16)


def head_mask(plan, k):
    lane = iota((1, plan.lanes), 1)
    return (lane >= k * plan.dim) & (lane < (k + 1) * plan.dim)


def spread(plan, columns):
    head, lane = iota((plan.heads, plan.width), 0), iota((plan.heads, plan.width), 1)
    ones = ((lane >= head * plan.dim) & (lane < (head + 1) * plan.dim)).astype(F32).astype(BF16)
    high = columns.astype(BF16)
    low = (columns - high.astype(F32)).astype(BF16)
    return dot(high, ones) + dot(low, ones)


def doc_edges(plan, lengths_ref, block_start):
    start = jnp.int32(0)
    last, first = jnp.int32(0), jnp.int32(2**30)
    for i in range(lengths_ref.shape[0]):
        last = jnp.where(start < block_start + plan.tokens, start, last)
        first = jnp.where(start >= block_start, jnp.minimum(first, start), first)
        start = start + lengths_ref[i]
    return last, first


def doc_index(lengths_ref, positions):
    start = jnp.int32(0)
    index = jnp.zeros(positions.shape, jnp.int32)
    for i in range(lengths_ref.shape[0]):
        index = index + (positions >= start).astype(jnp.int32)
        start = start + lengths_ref[i]
    return index


def exit_columns(plan, decay, last, block_start):
    after = tri(plan.tokens, lambda t, u: u > t)
    keep = block_start + iota((plan.tokens, plan.heads), 0) >= last
    return jnp.where(keep, jnp.exp(exact_dot(decay, after, NT, False)), 0.0)


def reach_columns(plan, decay, first, block_start):
    until = tri(plan.tokens, lambda t, u: u <= t)
    carry = block_start + iota((plan.tokens, plan.heads), 0) < first
    return jnp.where(carry, jnp.exp(exact_dot(decay, until, NT, False)), 0.0)


def decay_bias(plan, lengths_ref, block_start):
    n = plan.tokens
    t, s = iota((n, n), 0), iota((n, n), 1)
    same = doc_index(lengths_ref, t + block_start) == doc_index(lengths_ref, s + block_start)
    return jnp.where(same & (t >= s), math.log(plan.scale), NEVER)


def log_sums(plan, decay):
    until = tri(plan.tokens, lambda t, u: u <= t)
    return exact_dot(decay, until, NT, False), exact_dot(decay, until, NT, True)


def own_heads(plan, product, rows):
    out = product[:rows]
    for k in range(1, plan.group):
        out = jnp.where(head_mask(plan, k), product[k * rows : (k + 1) * rows], out)
    return out


def stack_heads(plan, x):
    return jnp.concatenate(
        [jnp.where(head_mask(plan, k), x, jnp.zeros_like(x)) for k in range(plan.group)], axis=0
    )


def windows(plan):
    for h in range(0, plan.group, 2):
        heads = range(h, min(h + 2, plan.group))
        start = heads[0] * plan.dim // 128 * 128
        yield heads, start, -(-(heads[-1] + 1) * plan.dim // 128) * 128


def block_diagonal(plan, x, heads, start, stop):
    zeros = lambda rows: [jnp.zeros((rows, stop - start), x.dtype)] if rows else []
    x = x[:, start:stop]
    lane = iota((1, stop - start), 1) + start
    parts = zeros(heads[0] * plan.dim - start)
    for h in heads:
        on = (lane >= h * plan.dim) & (lane < (h + 1) * plan.dim)
        parts.append(jnp.where(on, x, jnp.zeros_like(x)))
    parts += zeros(stop - (heads[-1] + 1) * plan.dim)
    return jnp.concatenate(parts, axis=0)


def sum_windows(plan, terms):
    tiles = [None] * (plan.lanes // 128)
    for start, stop, term in terms:
        for j in range(start // 128, stop // 128):
            tile = term[:, j * 128 - start : (j + 1) * 128 - start]
            tiles[j] = tile if tiles[j] is None else tiles[j] + tile
    return jnp.concatenate(tiles, axis=1)


def through_states(plan, x, state, dims):
    return sum_windows(
        plan,
        [
            (start, stop, dot(x[:, start:stop], block_diagonal(plan, state, heads, start, stop), dims))
            for heads, start, stop in windows(plan)
        ],
    )


def outer_states(plan, x, y):
    terms = []
    for heads, start, stop in windows(plan):
        product = dot(x[:, start:stop], y[:, start:stop], TN)
        lane = iota((1, stop - start), 1) + start
        out = jnp.zeros((plan.dim, stop - start), F32)
        for h in heads:
            on = (lane >= h * plan.dim) & (lane < (h + 1) * plan.dim)
            out = jnp.where(on, product[h * plan.dim - start : (h + 1) * plan.dim - start], out)
        terms.append((start, stop, out))
    return sum_windows(plan, terms)


def lanes_of(plan, g):
    return slice(g * plan.lanes, (g + 1) * plan.lanes)


def store_pieces(plan, mine, state_ref, piece_refs):
    for m, piece in zip(plan.out_masks, piece_refs):
        start = pl.multiple_of((mine ^ m) * plan.rows, plan.rows)
        for j in range(plan.tiles):
            piece[j * plan.rows : (j + 1) * plan.rows, :] = state_ref[
                pl.ds(start, plan.rows), j * 128 : (j + 1) * 128
            ]


def load_pieces(plan, own, piece_refs, state_ref):
    def at_place(mine):
        order = [piece_refs[plan.back_masks.index(mine ^ b)] for b in range(plan.pieces)]
        for j in range(plan.tiles):
            at = slice(j * plan.rows, (j + 1) * plan.rows)
            rows = jnp.concatenate([piece[at, :] for piece in order], axis=0)
            state_ref[:, j * 128 : (j + 1) * 128] = rows.astype(state_ref.dtype)

    for mine in range(plan.pieces):
        pl.when(own == mine)(functools.partial(at_place, mine))


def row_copies(source, target, sems):
    count = sems.shape[0]
    rows = source.shape[0] // count
    return [
        pltpu.make_async_copy(
            source.at[i * rows : (i + 1) * rows], target.at[i * rows : (i + 1) * rows], sems.at[i]
        )
        for i in range(count)
    ]


def exit_kernel(plan, lengths_hbm, decay_hbm, keys_hbm, values_hbm, *refs):
    pieces = refs[: plan.pieces]
    weighted_ref, lengths_ref, decay_ref, keys_ref, values_ref, state_ref, small_sems, key_sems, value_sems = refs[
        plan.pieces :
    ]
    lengths_copy = pltpu.make_async_copy(lengths_hbm, lengths_ref, small_sems.at[0])
    decay_copy = pltpu.make_async_copy(decay_hbm, decay_ref, small_sems.at[1])
    lengths_copy.start()
    decay_copy.start()
    keys_copies = row_copies(keys_hbm, keys_ref, key_sems)
    values_copies = row_copies(values_hbm, values_ref, value_sems)
    for copy in keys_copies + values_copies:
        copy.start()
    block_start, mine = place(plan)
    lengths_copy.wait()
    last, first = doc_edges(plan, lengths_ref, block_start)
    decay_copy.wait()
    decay = decay_ref[...]
    weights = spread(plan, exit_columns(plan, decay, last, block_start))
    whole = jnp.exp(jnp.sum(decay, axis=1, keepdims=True))
    whole = jnp.where(first >= block_start + plan.tokens, whole, 0.0)
    head = iota((plan.heads, 128), 0)
    rows = []
    for j in range(plan.tiles):
        lane = iota((plan.heads, 128), 1) + j * 128
        on = (lane >= head * plan.dim) & (lane < (head + 1) * plan.dim)
        rows.append(jnp.sum(jnp.where(on, whole, 0.0), axis=0, keepdims=True))
    rows.append(jnp.zeros((plan.factor_rows - plan.tiles, 128), F32))
    rows = jnp.concatenate(rows, axis=0)
    for piece in pieces:
        piece[plan.piece_rows :, :] = rows
    for copy in keys_copies:
        copy.wait()
    weighted_ref[...] = (keys_ref[...].astype(F32) * weights).astype(BF16)
    for copy in values_copies:
        copy.wait()
    for g in range(plan.groups):
        at = lanes_of(plan, g)
        state_ref[:, at] = outer_states(plan, weighted_ref[:, at], values_ref[:, at])
    store_pieces(plan, mine, state_ref, pieces)


def chain_kernel(plan, reverse, with_carry, groups, *refs):
    n, rows = plan.pieces, plan.rows
    pieces, factors = refs[:n], refs[n : 2 * n]
    hops = refs[2 * n : 2 * n + 2]
    outs = refs[2 * n + 2 :] if with_carry else refs[2 * n :]
    group = lax.axis_index("ctx") // n
    end = groups - 1 if reverse else 0
    by_first = lax.rem(group, 2) == (0 if reverse else 1)
    order = range(n - 1, -1, -1) if reverse else range(n)

    def at_place(mine):
        for j in range(plan.tiles):
            at = slice(j * rows, (j + 1) * rows)
            tile = None
            if with_carry:
                tile = jnp.where(group == end, 0.0, jnp.where(by_first, hops[0][at], hops[1][at]))
            for step, b in enumerate(order):
                m = plan.out_masks.index(mine ^ b)
                if with_carry:
                    outs[plan.back_masks.index(mine ^ b)][at] = tile
                    if step == n - 1:
                        break
                rate = factors[m][plan.piece_rows + j : plan.piece_rows + j + 1, :]
                tile = pieces[m][at] if tile is None else tile * rate + pieces[m][at]
            if not with_carry:
                outs[0][at] = tile

    own = place(plan)[1]
    for mine in range(n):
        pl.when(own == mine)(functools.partial(at_place, mine))


def local_kernel(
    plan,
    lengths_ref,
    decay_ref,
    queries_ref,
    keys_ref,
    values_ref,
    out_grad_ref,
    gain_ref,
    probs_ref,
    local_ref,
    reached_ref,
    scaled_ref,
):
    block_start = place(plan)[0]
    decay = decay_ref[...]
    last, first = doc_edges(plan, lengths_ref, block_start)
    columns, rows = log_sums(plan, decay)
    bias = decay_bias(plan, lengths_ref, block_start)
    carry = block_start + iota(columns.shape, 0) < first
    reach = spread(plan, jnp.where(carry, jnp.exp(columns), 0.0) * plan.scale)
    n = plan.tokens
    for g in range(plan.groups):
        at = lanes_of(plan, g)
        scaled_ref[:, at] = out_grad_ref[:, at].astype(F32) * gain_ref[:, at]
        queries, keys, values = queries_ref[:, at], keys_ref[:, at], values_ref[:, at]
        reached_ref[:, at] = (queries.astype(F32) * reach[:, at]).astype(BF16)
        scores = dot(stack_heads(plan, queries), keys, NT)
        probs = []
        for k in range(plan.group):
            h = g * plan.group + k
            mask = jnp.exp(columns[:, h : h + 1] - rows[h : h + 1, :] + bias)
            probs.append((scores[k * n : (k + 1) * n] * mask).astype(BF16))
        probs = jnp.concatenate(probs, axis=1)
        probs_ref[:, g * plan.group * n : (g + 1) * plan.group * n] = probs
        local_ref[:, at] = dot(probs, stack_heads(plan, values))


def attend_kernel(plan, local_ref, reached_ref, scaled_ref, *refs):
    pieces = refs[: plan.pieces]
    attended_ref, sums_ref, incoming_ref = refs[plan.pieces :]
    load_pieces(plan, place(plan)[1], pieces, incoming_ref)
    squares = inner = None
    for g in range(plan.groups):
        at = lanes_of(plan, g)
        incoming = incoming_ref[:, at]
        attended = local_ref[:, at] + through_states(plan, reached_ref[:, at], incoming, NN)
        attended_ref[:, at] = attended
        square, product = attended * attended, scaled_ref[:, at] * attended
        for j in range(0, plan.lanes, 128):
            squares = square[:, j : j + 128] if squares is None else squares + square[:, j : j + 128]
            inner = product[:, j : j + 128] if inner is None else inner + product[:, j : j + 128]
    lane = iota((plan.tokens, 128), 1)
    sums_ref[...] = jnp.where(
        lane < 64, jnp.sum(squares, axis=1, keepdims=True), jnp.sum(inner, axis=1, keepdims=True)
    )


def grad_kernel(
    plan, features, attended_ref, scaled_ref, sums_ref, other_ref, reached_ref, *refs
):
    pieces, (attended_grad_ref, norm_ref, state_ref) = refs[: plan.pieces], refs[plan.pieces :]
    sums = sums_ref[...] + other_ref[...]
    inverse = lax.rsqrt(sums[:, :1] / features + EPSILON)
    norm_ref[...] = jnp.broadcast_to(inverse, norm_ref.shape)
    slope = inverse * inverse * inverse * sums[:, 64:65] / features
    for g in range(plan.groups):
        at = lanes_of(plan, g)
        attended_grad = (scaled_ref[:, at] * inverse - attended_ref[:, at] * slope).astype(BF16)
        attended_grad_ref[:, at] = attended_grad
        state_ref[:, at] = outer_states(plan, reached_ref[:, at], attended_grad)
    store_pieces(plan, place(plan)[1], state_ref, pieces)


def inner_kernel(
    plan,
    lengths_ref,
    decay_ref,
    queries_ref,
    keys_ref,
    values_ref,
    gain_ref,
    attended_ref,
    attended_grad_ref,
    norm_ref,
    probs_ref,
    incoming_ref,
    output_ref,
    query_grad_ref,
    key_local_ref,
    value_local_ref,
    weighted_ref,
):
    block_start = place(plan)[0]
    decay = decay_ref[...]
    last, first = doc_edges(plan, lengths_ref, block_start)
    columns, rows = log_sums(plan, decay)
    bias = decay_bias(plan, lengths_ref, block_start)
    position = block_start + iota(columns.shape, 0)
    reach = spread(plan, jnp.where(position < first, jnp.exp(columns), 0.0) * plan.scale)
    exits = spread(plan, exit_columns(plan, decay, last, block_start))
    norm = norm_ref[:, :1]
    n = plan.tokens
    for g in range(plan.groups):
        at = lanes_of(plan, g)
        output_ref[:, at] = (attended_ref[:, at] * norm * gain_ref[:, at]).astype(BF16)
        queries, keys, values = queries_ref[:, at], keys_ref[:, at], values_ref[:, at]
        grads = attended_grad_ref[:, at]
        weighted_ref[:, at] = (values.astype(F32) * exits[:, at]).astype(BF16)
        scores = dot(stack_heads(plan, grads), values, NT)
        score_grads = []
        for k in range(plan.group):
            h = g * plan.group + k
            mask = jnp.exp(columns[:, h : h + 1] - rows[h : h + 1, :] + bias)
            score_grads.append((scores[k * n : (k + 1) * n] * mask).astype(BF16))
        score_grads = jnp.concatenate(score_grads, axis=1)
        probs = probs_ref[:, g * plan.group * n : (g + 1) * plan.group * n]
        query_grad = dot(score_grads, stack_heads(plan, keys))
        query_grad += reach[:, at] * through_states(plan, grads, incoming_ref[:, at], NT)
        query_grad_ref[:, at] = query_grad.astype(BF16)
        key_local_ref[:, at] = own_heads(plan, dot(score_grads, queries, TN), n)
        value_local_ref[:, at] = own_heads(plan, dot(probs, grads, TN), n)


def finish_kernel(
    plan, key_local_ref, value_local_ref, weighted_values_ref, weighted_keys_ref, *refs
):
    pieces = refs[: plan.pieces]
    key_grad_hbm, value_grad_hbm, state_ref, key_grad_ref, value_grad_ref, key_sems, value_sems = refs[
        plan.pieces :
    ]
    load_pieces(plan, place(plan)[1], pieces, state_ref)
    copies = []
    for g in range(plan.groups):
        at = lanes_of(plan, g)
        later = state_ref[:, at]
        key_grad = key_local_ref[:, at] + through_states(plan, weighted_values_ref[:, at], later, NT)
        key_grad_ref[:, at] = key_grad.astype(BF16)
        copies.append(
            pltpu.make_async_copy(key_grad_ref.at[:, at], key_grad_hbm.at[:, at], key_sems.at[g])
        )
        copies[-1].start()
        value_grad = value_local_ref[:, at] + through_states(plan, weighted_keys_ref[:, at], later, NN)
        value_grad_ref[:, at] = value_grad.astype(BF16)
        copies.append(
            pltpu.make_async_copy(value_grad_ref.at[:, at], value_grad_hbm.at[:, at], value_sems.at[g])
        )
        copies[-1].start()
    for copy in copies:
        copy.wait()


SCALAR = pl.BlockSpec(memory_space=pltpu.SMEM)
WHOLE = pl.BlockSpec(memory_space=pltpu.VMEM)
FAR = pl.BlockSpec(memory_space=pltpu.HBM)


def call(kernel, name, scalars, arrays, outs, scratch=(), flops=0, far_in=0, far_out=False):
    scalars = [pltpu.with_memory_space_constraint(a, pltpu.HBM) for a in scalars]
    arrays = [
        pltpu.with_memory_space_constraint(a, pltpu.HBM) if i < far_in else a for i, a in enumerate(arrays)
    ]
    moved = sum(a.size * a.dtype.itemsize for a in (*arrays, *outs))
    return pl.pallas_call(
        kernel,
        name=name,
        out_shape=outs,
        in_specs=[SCALAR] * len(scalars) + [FAR] * far_in + [WHOLE] * (len(arrays) - far_in),
        out_specs=[FAR if far_out else WHOLE] * len(outs),
        scratch_shapes=list(scratch),
        compiler_params=pltpu.CompilerParams(vmem_limit_bytes=40 * 2**20),
        cost_estimate=pl.CostEstimate(flops=flops, bytes_accessed=moved, transcendentals=0),
    )(*scalars, *arrays)


def array(*shape, dtype=F32):
    return jax.ShapeDtypeStruct(shape, dtype)


def exchange(pieces, count, masks):
    return [
        lax.ppermute(piece, "ctx", [(i, i ^ m) for i in range(count)]) if m else piece
        for m, piece in zip(masks, pieces)
    ]


def shift(x, count, by):
    pairs = [(i, i + by) for i in range(count) if 0 <= i + by < count]
    return lax.ppermute(x, "ctx", pairs)


def group_swaps(n, count):
    first = [(i, i ^ n) for i in range(count)]
    second = [(i, i ^ 1 if i < n or i >= count - n else (((i // n - 1) ^ 1) + 1) * n + i % n) for i in range(count)]
    return first, second


def scan_whole(plan, state, factor, count, reach, sign):
    held = shift(state, count, sign)
    rates = shift(factor, count, sign)
    by = 1
    while by < reach:
        held = held + rates * shift(held, count, sign * by)
        rates = rates * shift(rates, count, sign * by)
        by *= 2
    return held


def on_device(queries, keys, values, decay_log, norm_gain, out_grad, doc_lengths):
    tokens, width = queries.shape
    heads = decay_log.shape[0]
    count = lax.axis_size("ctx")
    features = width * lax.axis_size("head")
    reach = count // 4
    even = reach > 1 and reach & (reach - 1) == 0 and (width // heads) % (8 * reach) == 0
    plan = Plan(tokens, width, heads, reach if even else 1)
    n = plan.pieces
    gain = norm_gain.reshape(1, width)
    like = array(tokens, width, dtype=BF16)
    wide = array(tokens, width)
    state = pltpu.VMEM((plan.dim, width), F32)
    piece = array(plan.piece_rows, 128)
    framed = array(plan.piece_rows + plan.factor_rows, 128)

    *pieces, weighted_keys = call(
        functools.partial(exit_kernel, plan),
        "exit_states",
        (),
        (doc_lengths, decay_log, keys, values),
        [framed] * n + [like],
        [
            pltpu.SMEM(doc_lengths.shape, jnp.int32),
            pltpu.VMEM(decay_log.shape, F32),
            pltpu.VMEM((tokens, width), BF16),
            pltpu.VMEM((tokens, width), BF16),
            state,
            pltpu.SemaphoreType.DMA((2,)),
            pltpu.SemaphoreType.DMA((1,)),
            pltpu.SemaphoreType.DMA((1,)),
        ],
        flops=10**8,
        far_in=4,
    )
    if even:
        pieces = exchange(pieces, count, plan.out_masks)
    frames = pieces

    def chain(pieces, reverse, carry=None):
        with_carry = carry is not None
        return call(
            functools.partial(chain_kernel, plan, reverse, with_carry, count // n),
            "prefix_states" if with_carry else "total_state",
            (),
            (*pieces, *frames, *carry) if with_carry else (*pieces, *frames),
            [piece] * n if with_carry else [piece],
        )

    def entering(pieces, reverse):
        sign = -1 if reverse else 1
        if not even:
            whole = pieces[0][: plan.piece_rows].reshape(plan.tiles, plan.rows, 128)
            factor = frames[0][plan.piece_rows : plan.piece_rows + plan.tiles, None, :]
            return [scan_whole(plan, whole, factor, count, reach, sign).reshape(piece.shape)]
        (total,) = chain(pieces, reverse)
        carry = [lax.ppermute(total, "ctx", pairs) for pairs in group_swaps(n, count)]
        return exchange(chain(pieces, reverse, carry), count, plan.back_masks)

    incoming = entering(pieces, False)
    probs, local, reached, scaled = call(
        functools.partial(local_kernel, plan),
        "local_attention",
        (doc_lengths,),
        (decay_log, queries, keys, values, out_grad, gain),
        [array(tokens, heads * tokens, dtype=BF16), wide, like, wide],
        flops=10**9,
    )
    attended, sums, incoming_state = call(
        functools.partial(attend_kernel, plan),
        "attended",
        (),
        (local, reached, scaled, *incoming),
        [wide, array(tokens, 128), array(plan.dim, width, dtype=BF16)],
    )
    other = lax.ppermute(sums, "head", [(0, 1), (1, 0)])
    *pieces, attended_grad, norm = call(
        functools.partial(grad_kernel, plan, features),
        "attended_grad",
        (),
        (attended, scaled, sums, other, reached),
        [piece] * n + [like, array(tokens, 128)],
        [state],
    )
    if even:
        pieces = exchange(pieces, count, plan.out_masks)
    later = entering(pieces, True)
    output, query_grad, key_local, value_local, weighted_values = call(
        functools.partial(inner_kernel, plan),
        "local_grads",
        (doc_lengths,),
        (
            decay_log,
            queries,
            keys,
            values,
            gain,
            attended,
            attended_grad,
            norm,
            probs,
            incoming_state,
        ),
        [like, like, wide, wide, like],
        flops=10**9,
    )
    key_grad, value_grad = call(
        functools.partial(finish_kernel, plan),
        "key_value_grads",
        (),
        (key_local, value_local, weighted_values, weighted_keys, *later),
        [like, like],
        [
            pltpu.VMEM((plan.dim, width), BF16),
            pltpu.VMEM((tokens, width), BF16),
            pltpu.VMEM((tokens, width), BF16),
            pltpu.SemaphoreType.DMA((plan.groups,)),
            pltpu.SemaphoreType.DMA((plan.groups,)),
        ],
        far_out=True,
    )
    return (output, query_grad, key_grad, value_grad)


def solution(mesh):
    in_specs = (
        P("ctx", "head"),
        P("ctx", "head"),
        P("ctx", "head"),
        P("head", "ctx"),
        P("head"),
        P("ctx", "head"),
        P(),
    )
    out_specs = (P("ctx", "head"), P("ctx", "head"), P("ctx", "head"), P("ctx", "head"))
    return jax.shard_map(
        on_device, mesh=mesh, in_specs=in_specs, out_specs=out_specs, check_vma=False
    )
```

```python
import functools
import math

import jax
import jax.numpy as jnp
from jax import lax
from jax.experimental import pallas as pl
from jax.experimental.pallas import tpu as pltpu
from jax.sharding import PartitionSpec as P

EPSILON = 1e-06
NEVER = -1e30
F32 = jnp.float32
BF16 = jnp.bfloat16
NN = (((1,), (0,)), ((), ()))
NT = (((1,), (1,)), ((), ()))
TN = (((0,), (0,)), ((), ()))


def dot(a, b, dims=NN):
    return lax.dot_general(a, b, dims, preferred_element_type=F32)


def split3(x):
    a = x.astype(BF16)
    rest = x - a.astype(F32)
    b = rest.astype(BF16)
    return a, b, (rest - b.astype(F32)).astype(BF16)


def exact_dot(x, ones, dims, x_first):
    out = None
    for part in split3(x):
        term = dot(part, ones, dims) if x_first else dot(ones, part, dims)
        out = term if out is None else out + term
    return out


class Plan:
    def __init__(self, tokens, width, heads, pieces):
        self.tokens, self.width, self.heads = tokens, width, heads
        self.dim = width // heads
        self.group = math.lcm(self.dim, 128) // self.dim
        self.lanes = self.group * self.dim
        self.groups = heads // self.group
        self.pieces = pieces
        self.out_masks = tuple(range(pieces))
        self.back_masks = (0, *range(pieces - 1, 0, -1))
        self.rows = self.dim // pieces
        self.tiles = width // 128
        self.scale = 1.0 / math.sqrt(self.dim)
        self.piece_rows = self.tiles * self.rows
        self.factor_rows = -(-self.tiles // 8) * 8


def place(plan):
    index = lax.axis_index("ctx")
    return index * plan.tokens, lax.rem(index, plan.pieces)


def iota(shape, dim):
    return lax.broadcasted_iota(jnp.int32, shape, dim)


def tri(n, keep):
    return keep(iota((n, n), 0), iota((n, n), 1)).astype(F32).astype(BF16)


def head_mask(plan, k):
    lane = iota((1, plan.lanes), 1)
    return (lane >= k * plan.dim) & (lane < (k + 1) * plan.dim)


def spread(plan, columns):
    head, lane = iota((plan.heads, plan.width), 0), iota((plan.heads, plan.width), 1)
    ones = ((lane >= head * plan.dim) & (lane < (head + 1) * plan.dim)).astype(F32).astype(BF16)
    high = columns.astype(BF16)
    low = (columns - high.astype(F32)).astype(BF16)
    return dot(high, ones) + dot(low, ones)


def doc_edges(plan, lengths_ref, block_start):
    start = jnp.int32(0)
    last, first = jnp.int32(0), jnp.int32(2**30)
    for i in range(lengths_ref.shape[0]):
        last = jnp.where(start < block_start + plan.tokens, start, last)
        first = jnp.where(start >= block_start, jnp.minimum(first, start), first)
        start = start + lengths_ref[i]
    return last, first


def doc_index(lengths_ref, positions):
    start = jnp.int32(0)
    index = jnp.zeros(positions.shape, jnp.int32)
    for i in range(lengths_ref.shape[0]):
        index = index + (positions >= start).astype(jnp.int32)
        start = start + lengths_ref[i]
    return index


def exit_columns(plan, decay, last, block_start):
    after = tri(plan.tokens, lambda t, u: u > t)
    keep = block_start + iota((plan.tokens, plan.heads), 0) >= last
    return jnp.where(keep, jnp.exp(exact_dot(decay, after, NT, False)), 0.0)


def reach_columns(plan, decay, first, block_start):
    until = tri(plan.tokens, lambda t, u: u <= t)
    carry = block_start + iota((plan.tokens, plan.heads), 0) < first
    return jnp.where(carry, jnp.exp(exact_dot(decay, until, NT, False)), 0.0)


def decay_bias(plan, lengths_ref, block_start):
    n = plan.tokens
    t, s = iota((n, n), 0), iota((n, n), 1)
    same = doc_index(lengths_ref, t + block_start) == doc_index(lengths_ref, s + block_start)
    return jnp.where(same & (t >= s), math.log(plan.scale), NEVER)


def log_sums(plan, decay):
    until = tri(plan.tokens, lambda t, u: u <= t)
    return exact_dot(decay, until, NT, False), exact_dot(decay, until, NT, True)


def own_heads(plan, product, rows):
    out = product[:rows]
    for k in range(1, plan.group):
        out = jnp.where(head_mask(plan, k), product[k * rows : (k + 1) * rows], out)
    return out


def stack_heads(plan, x):
    return jnp.concatenate(
        [jnp.where(head_mask(plan, k), x, jnp.zeros_like(x)) for k in range(plan.group)], axis=0
    )


def windows(plan):
    for h in range(0, plan.group, 2):
        heads = range(h, min(h + 2, plan.group))
        start = heads[0] * plan.dim // 128 * 128
        yield heads, start, -(-(heads[-1] + 1) * plan.dim // 128) * 128


def block_diagonal(plan, x, heads, start, stop):
    zeros = lambda rows: [jnp.zeros((rows, stop - start), x.dtype)] if rows else []
    x = x[:, start:stop]
    lane = iota((1, stop - start), 1) + start
    parts = zeros(heads[0] * plan.dim - start)
    for h in heads:
        on = (lane >= h * plan.dim) & (lane < (h + 1) * plan.dim)
        parts.append(jnp.where(on, x, jnp.zeros_like(x)))
    parts += zeros(stop - (heads[-1] + 1) * plan.dim)
    return jnp.concatenate(parts, axis=0)


def sum_windows(plan, terms):
    tiles = [None] * (plan.lanes // 128)
    for start, stop, term in terms:
        for j in range(start // 128, stop // 128):
            tile = term[:, j * 128 - start : (j + 1) * 128 - start]
            tiles[j] = tile if tiles[j] is None else tiles[j] + tile
    return jnp.concatenate(tiles, axis=1)


def through_states(plan, x, state, dims):
    return sum_windows(
        plan,
        [
            (start, stop, dot(x[:, start:stop], block_diagonal(plan, state, heads, start, stop), dims))
            for heads, start, stop in windows(plan)
        ],
    )


def outer_states(plan, x, y):
    terms = []
    for heads, start, stop in windows(plan):
        product = dot(x[:, start:stop], y[:, start:stop], TN)
        lane = iota((1, stop - start), 1) + start
        out = jnp.zeros((plan.dim, stop - start), F32)
        for h in heads:
            on = (lane >= h * plan.dim) & (lane < (h + 1) * plan.dim)
            out = jnp.where(on, product[h * plan.dim - start : (h + 1) * plan.dim - start], out)
        terms.append((start, stop, out))
    return sum_windows(plan, terms)


def lanes_of(plan, g):
    return slice(g * plan.lanes, (g + 1) * plan.lanes)


def store_pieces(plan, mine, state_ref, piece_refs):
    for m, piece in zip(plan.out_masks, piece_refs):
        start = pl.multiple_of((mine ^ m) * plan.rows, plan.rows)
        for j in range(plan.tiles):
            piece[j * plan.rows : (j + 1) * plan.rows, :] = state_ref[
                pl.ds(start, plan.rows), j * 128 : (j + 1) * 128
            ]


def load_pieces(plan, mine, piece_refs, state_ref):
    for m, piece in zip(plan.back_masks, piece_refs):
        start = pl.multiple_of((mine ^ m) * plan.rows, plan.rows)
        for j in range(plan.tiles):
            state_ref[pl.ds(start, plan.rows), j * 128 : (j + 1) * 128] = piece[
                j * plan.rows : (j + 1) * plan.rows, :
            ]


def row_copies(source, target, sems):
    count = sems.shape[0]
    rows = source.shape[0] // count
    return [
        pltpu.make_async_copy(
            source.at[i * rows : (i + 1) * rows], target.at[i * rows : (i + 1) * rows], sems.at[i]
        )
        for i in range(count)
    ]


def exit_kernel(plan, lengths_hbm, decay_hbm, keys_hbm, values_hbm, *refs):
    pieces = refs[: plan.pieces]
    weighted_ref, lengths_ref, decay_ref, keys_ref, values_ref, state_ref, small_sems, key_sems, value_sems = refs[
        plan.pieces :
    ]
    lengths_copy = pltpu.make_async_copy(lengths_hbm, lengths_ref, small_sems.at[0])
    decay_copy = pltpu.make_async_copy(decay_hbm, decay_ref, small_sems.at[1])
    lengths_copy.start()
    decay_copy.start()
    keys_copies = row_copies(keys_hbm, keys_ref, key_sems)
    values_copies = row_copies(values_hbm, values_ref, value_sems)
    for copy in keys_copies + values_copies:
        copy.start()
    block_start, mine = place(plan)
    lengths_copy.wait()
    last, first = doc_edges(plan, lengths_ref, block_start)
    decay_copy.wait()
    decay = decay_ref[...]
    weights = spread(plan, exit_columns(plan, decay, last, block_start))
    whole = jnp.exp(jnp.sum(decay, axis=1, keepdims=True))
    whole = jnp.where(first >= block_start + plan.tokens, whole, 0.0)
    head = iota((plan.heads, 128), 0)
    rows = []
    for j in range(plan.tiles):
        lane = iota((plan.heads, 128), 1) + j * 128
        on = (lane >= head * plan.dim) & (lane < (head + 1) * plan.dim)
        rows.append(jnp.sum(jnp.where(on, whole, 0.0), axis=0, keepdims=True))
    rows.append(jnp.zeros((plan.factor_rows - plan.tiles, 128), F32))
    rows = jnp.concatenate(rows, axis=0)
    for piece in pieces:
        piece[plan.piece_rows :, :] = rows
    for copy in keys_copies:
        copy.wait()
    weighted_ref[...] = (keys_ref[...].astype(F32) * weights).astype(BF16)
    for copy in values_copies:
        copy.wait()
    for g in range(plan.groups):
        at = lanes_of(plan, g)
        state_ref[:, at] = outer_states(plan, weighted_ref[:, at], values_ref[:, at])
    store_pieces(plan, mine, state_ref, pieces)


def chain_kernel(plan, reverse, with_carry, groups, *refs):
    n, rows = plan.pieces, plan.rows
    pieces, factors = refs[:n], refs[n : 2 * n]
    hops = refs[2 * n : 2 * n + 2]
    outs = refs[2 * n + 2 :] if with_carry else refs[2 * n :]
    group = lax.axis_index("ctx") // n
    end = groups - 1 if reverse else 0
    by_first = lax.rem(group, 2) == (0 if reverse else 1)
    order = range(n - 1, -1, -1) if reverse else range(n)

    def at_place(mine):
        for j in range(plan.tiles):
            at = slice(j * rows, (j + 1) * rows)
            tile = None
            if with_carry:
                tile = jnp.where(group == end, 0.0, jnp.where(by_first, hops[0][at], hops[1][at]))
            for step, b in enumerate(order):
                m = plan.out_masks.index(mine ^ b)
                if with_carry:
                    outs[plan.back_masks.index(mine ^ b)][at] = tile
                    if step == n - 1:
                        break
                rate = factors[m][plan.piece_rows + j : plan.piece_rows + j + 1, :]
                tile = pieces[m][at] if tile is None else tile * rate + pieces[m][at]
            if not with_carry:
                outs[0][at] = tile

    own = place(plan)[1]
    for mine in range(n):
        pl.when(own == mine)(functools.partial(at_place, mine))


def local_kernel(
    plan, lengths_ref, decay_ref, queries_ref, keys_ref, values_ref, probs_ref, local_ref, reached_ref
):
    block_start = place(plan)[0]
    decay = decay_ref[...]
    last, first = doc_edges(plan, lengths_ref, block_start)
    columns, rows = log_sums(plan, decay)
    bias = decay_bias(plan, lengths_ref, block_start)
    carry = block_start + iota(columns.shape, 0) < first
    reach = spread(plan, jnp.where(carry, jnp.exp(columns), 0.0) * plan.scale)
    n = plan.tokens
    for g in range(plan.groups):
        at = lanes_of(plan, g)
        queries, keys, values = queries_ref[:, at], keys_ref[:, at], values_ref[:, at]
        reached_ref[:, at] = (queries.astype(F32) * reach[:, at]).astype(BF16)
        scores = dot(stack_heads(plan, queries), keys, NT)
        probs = []
        for k in range(plan.group):
            h = g * plan.group + k
            mask = jnp.exp(columns[:, h : h + 1] - rows[h : h + 1, :] + bias)
            probs.append((scores[k * n : (k + 1) * n] * mask).astype(BF16))
        probs = jnp.concatenate(probs, axis=1)
        probs_ref[:, g * plan.group * n : (g + 1) * plan.group * n] = probs
        local_ref[:, at] = dot(probs, stack_heads(plan, values))


def attend_kernel(plan, local_ref, reached_ref, out_grad_ref, gain_ref, *refs):
    pieces = refs[: plan.pieces]
    attended_ref, sums_ref, incoming_ref, state_ref = refs[plan.pieces :]
    load_pieces(plan, place(plan)[1], pieces, state_ref)
    squares = inner = None
    for g in range(plan.groups):
        at = lanes_of(plan, g)
        incoming = state_ref[:, at].astype(BF16)
        incoming_ref[:, at] = incoming
        attended = local_ref[:, at] + through_states(plan, reached_ref[:, at], incoming, NN)
        attended_ref[:, at] = attended
        grad = out_grad_ref[:, at].astype(F32) * gain_ref[:, at]
        square, product = attended * attended, grad * attended
        for j in range(0, plan.lanes, 128):
            squares = square[:, j : j + 128] if squares is None else squares + square[:, j : j + 128]
            inner = product[:, j : j + 128] if inner is None else inner + product[:, j : j + 128]
    lane = iota((plan.tokens, 128), 1)
    sums_ref[...] = jnp.where(
        lane < 64, jnp.sum(squares, axis=1, keepdims=True), jnp.sum(inner, axis=1, keepdims=True)
    )


def grad_kernel(
    plan, features, attended_ref, out_grad_ref, gain_ref, sums_ref, other_ref, reached_ref, *refs
):
    pieces, (attended_grad_ref, norm_ref, state_ref) = refs[: plan.pieces], refs[plan.pieces :]
    sums = sums_ref[...] + other_ref[...]
    inverse = lax.rsqrt(sums[:, :1] / features + EPSILON)
    norm_ref[...] = jnp.broadcast_to(inverse, norm_ref.shape)
    slope = inverse * inverse * inverse * sums[:, 64:65] / features
    for g in range(plan.groups):
        at = lanes_of(plan, g)
        grad = out_grad_ref[:, at].astype(F32) * gain_ref[:, at]
        attended_grad = (grad * inverse - attended_ref[:, at] * slope).astype(BF16)
        attended_grad_ref[:, at] = attended_grad
        state_ref[:, at] = outer_states(plan, reached_ref[:, at], attended_grad)
    store_pieces(plan, place(plan)[1], state_ref, pieces)


def inner_kernel(
    plan,
    lengths_ref,
    decay_ref,
    queries_ref,
    keys_ref,
    values_ref,
    gain_ref,
    attended_ref,
    attended_grad_ref,
    norm_ref,
    probs_ref,
    incoming_ref,
    output_ref,
    query_grad_ref,
    key_local_ref,
    value_local_ref,
    weighted_ref,
):
    block_start = place(plan)[0]
    decay = decay_ref[...]
    last, first = doc_edges(plan, lengths_ref, block_start)
    columns, rows = log_sums(plan, decay)
    bias = decay_bias(plan, lengths_ref, block_start)
    position = block_start + iota(columns.shape, 0)
    reach = spread(plan, jnp.where(position < first, jnp.exp(columns), 0.0) * plan.scale)
    exits = spread(plan, exit_columns(plan, decay, last, block_start))
    norm = norm_ref[:, :1]
    n = plan.tokens
    for g in range(plan.groups):
        at = lanes_of(plan, g)
        output_ref[:, at] = (attended_ref[:, at] * norm * gain_ref[:, at]).astype(BF16)
        queries, keys, values = queries_ref[:, at], keys_ref[:, at], values_ref[:, at]
        grads = attended_grad_ref[:, at]
        weighted_ref[:, at] = (values.astype(F32) * exits[:, at]).astype(BF16)
        scores = dot(stack_heads(plan, grads), values, NT)
        score_grads = []
        for k in range(plan.group):
            h = g * plan.group + k
            mask = jnp.exp(columns[:, h : h + 1] - rows[h : h + 1, :] + bias)
            score_grads.append((scores[k * n : (k + 1) * n] * mask).astype(BF16))
        score_grads = jnp.concatenate(score_grads, axis=1)
        probs = probs_ref[:, g * plan.group * n : (g + 1) * plan.group * n]
        query_grad = dot(score_grads, stack_heads(plan, keys))
        query_grad += reach[:, at] * through_states(plan, grads, incoming_ref[:, at], NT)
        query_grad_ref[:, at] = query_grad.astype(BF16)
        key_local_ref[:, at] = own_heads(plan, dot(score_grads, queries, TN), n)
        value_local_ref[:, at] = own_heads(plan, dot(probs, grads, TN), n)


def finish_kernel(
    plan, key_local_ref, value_local_ref, weighted_values_ref, weighted_keys_ref, *refs
):
    pieces = refs[: plan.pieces]
    key_grad_hbm, value_grad_hbm, state_ref, key_grad_ref, value_grad_ref, key_sems, value_sems = refs[
        plan.pieces :
    ]
    load_pieces(plan, place(plan)[1], pieces, state_ref)
    copies = []
    for g in range(plan.groups):
        at = lanes_of(plan, g)
        later = state_ref[:, at].astype(BF16)
        key_grad = key_local_ref[:, at] + through_states(plan, weighted_values_ref[:, at], later, NT)
        key_grad_ref[:, at] = key_grad.astype(BF16)
        copies.append(
            pltpu.make_async_copy(key_grad_ref.at[:, at], key_grad_hbm.at[:, at], key_sems.at[g])
        )
        copies[-1].start()
        value_grad = value_local_ref[:, at] + through_states(plan, weighted_keys_ref[:, at], later, NN)
        value_grad_ref[:, at] = value_grad.astype(BF16)
        copies.append(
            pltpu.make_async_copy(value_grad_ref.at[:, at], value_grad_hbm.at[:, at], value_sems.at[g])
        )
        copies[-1].start()
    for copy in copies:
        copy.wait()


SCALAR = pl.BlockSpec(memory_space=pltpu.SMEM)
WHOLE = pl.BlockSpec(memory_space=pltpu.VMEM)
FAR = pl.BlockSpec(memory_space=pltpu.HBM)


def call(kernel, name, scalars, arrays, outs, scratch=(), flops=0, far_in=0, far_out=False):
    scalars = [pltpu.with_memory_space_constraint(a, pltpu.HBM) for a in scalars]
    arrays = [
        pltpu.with_memory_space_constraint(a, pltpu.HBM) if i < far_in else a for i, a in enumerate(arrays)
    ]
    moved = sum(a.size * a.dtype.itemsize for a in (*arrays, *outs))
    return pl.pallas_call(
        kernel,
        name=name,
        out_shape=outs,
        in_specs=[SCALAR] * len(scalars) + [FAR] * far_in + [WHOLE] * (len(arrays) - far_in),
        out_specs=[FAR if far_out else WHOLE] * len(outs),
        scratch_shapes=list(scratch),
        compiler_params=pltpu.CompilerParams(vmem_limit_bytes=40 * 2**20),
        cost_estimate=pl.CostEstimate(flops=flops, bytes_accessed=moved, transcendentals=0),
    )(*scalars, *arrays)


def array(*shape, dtype=F32):
    return jax.ShapeDtypeStruct(shape, dtype)


def exchange(pieces, count, masks):
    return [
        lax.ppermute(piece, "ctx", [(i, i ^ m) for i in range(count)]) if m else piece
        for m, piece in zip(masks, pieces)
    ]


def shift(x, count, by):
    pairs = [(i, i + by) for i in range(count) if 0 <= i + by < count]
    return lax.ppermute(x, "ctx", pairs)


def group_swaps(n, count):
    first = [(i, i ^ n) for i in range(count)]
    second = [(i, i ^ 1 if i < n or i >= count - n else (((i // n - 1) ^ 1) + 1) * n + i % n) for i in range(count)]
    return first, second


def scan_whole(plan, state, factor, count, reach, sign):
    held = shift(state, count, sign)
    rates = shift(factor, count, sign)
    by = 1
    while by < reach:
        held = held + rates * shift(held, count, sign * by)
        rates = rates * shift(rates, count, sign * by)
        by *= 2
    return held


def on_device(queries, keys, values, decay_log, norm_gain, out_grad, doc_lengths):
    tokens, width = queries.shape
    heads = decay_log.shape[0]
    count = lax.axis_size("ctx")
    features = width * lax.axis_size("head")
    reach = count // 4
    even = reach > 1 and reach & (reach - 1) == 0 and (width // heads) % (8 * reach) == 0
    plan = Plan(tokens, width, heads, reach if even else 1)
    n = plan.pieces
    gain = norm_gain.reshape(1, width)
    like = array(tokens, width, dtype=BF16)
    wide = array(tokens, width)
    state = pltpu.VMEM((plan.dim, width), F32)
    piece = array(plan.piece_rows, 128)
    framed = array(plan.piece_rows + plan.factor_rows, 128)

    *pieces, weighted_keys = call(
        functools.partial(exit_kernel, plan),
        "exit_states",
        (),
        (doc_lengths, decay_log, keys, values),
        [framed] * n + [like],
        [
            pltpu.SMEM(doc_lengths.shape, jnp.int32),
            pltpu.VMEM(decay_log.shape, F32),
            pltpu.VMEM((tokens, width), BF16),
            pltpu.VMEM((tokens, width), BF16),
            state,
            pltpu.SemaphoreType.DMA((2,)),
            pltpu.SemaphoreType.DMA((1,)),
            pltpu.SemaphoreType.DMA((1,)),
        ],
        flops=10**8,
        far_in=4,
    )
    if even:
        pieces = exchange(pieces, count, plan.out_masks)
    frames = pieces

    def chain(pieces, reverse, carry=None):
        with_carry = carry is not None
        return call(
            functools.partial(chain_kernel, plan, reverse, with_carry, count // n),
            "prefix_states" if with_carry else "total_state",
            (),
            (*pieces, *frames, *carry) if with_carry else (*pieces, *frames),
            [piece] * n if with_carry else [piece],
        )

    def entering(pieces, reverse):
        sign = -1 if reverse else 1
        if not even:
            whole = pieces[0][: plan.piece_rows].reshape(plan.tiles, plan.rows, 128)
            factor = frames[0][plan.piece_rows : plan.piece_rows + plan.tiles, None, :]
            return [scan_whole(plan, whole, factor, count, reach, sign).reshape(piece.shape)]
        (total,) = chain(pieces, reverse)
        carry = [lax.ppermute(total, "ctx", pairs) for pairs in group_swaps(n, count)]
        return exchange(chain(pieces, reverse, carry), count, plan.back_masks)

    incoming = entering(pieces, False)
    probs, local, reached = call(
        functools.partial(local_kernel, plan),
        "local_attention",
        (doc_lengths,),
        (decay_log, queries, keys, values),
        [array(tokens, heads * tokens, dtype=BF16), wide, like],
        flops=10**9,
    )
    attended, sums, incoming_state = call(
        functools.partial(attend_kernel, plan),
        "attended",
        (),
        (local, reached, out_grad, gain, *incoming),
        [wide, array(tokens, 128), array(plan.dim, width, dtype=BF16)],
        [state],
    )
    other = lax.ppermute(sums, "head", [(0, 1), (1, 0)])
    *pieces, attended_grad, norm = call(
        functools.partial(grad_kernel, plan, features),
        "attended_grad",
        (),
        (attended, out_grad, gain, sums, other, reached),
        [piece] * n + [like, array(tokens, 128)],
        [state],
    )
    if even:
        pieces = exchange(pieces, count, plan.out_masks)
    later = entering(pieces, True)
    output, query_grad, key_local, value_local, weighted_values = call(
        functools.partial(inner_kernel, plan),
        "local_grads",
        (doc_lengths,),
        (
            decay_log,
            queries,
            keys,
            values,
            gain,
            attended,
            attended_grad,
            norm,
            probs,
            incoming_state,
        ),
        [like, like, wide, wide, like],
        flops=10**9,
    )
    key_grad, value_grad = call(
        functools.partial(finish_kernel, plan),
        "key_value_grads",
        (),
        (key_local, value_local, weighted_values, weighted_keys, *later),
        [like, like],
        [
            state,
            pltpu.VMEM((tokens, width), BF16),
            pltpu.VMEM((tokens, width), BF16),
            pltpu.SemaphoreType.DMA((plan.groups,)),
            pltpu.SemaphoreType.DMA((plan.groups,)),
        ],
        far_out=True,
    )
    return (output, query_grad, key_grad, value_grad)


def solution(mesh):
    in_specs = (
        P("ctx", "head"),
        P("ctx", "head"),
        P("ctx", "head"),
        P("head", "ctx"),
        P("head"),
        P("ctx", "head"),
        P(),
    )
    out_specs = (P("ctx", "head"), P("ctx", "head"), P("ctx", "head"), P("ctx", "head"))
    return jax.shard_map(
        on_device, mesh=mesh, in_specs=in_specs, out_specs=out_specs, check_vma=False
    )
```
